256 devices in a mesh: clip: 64 (over x_hi, y, z), frame: 4 (over x_lo, core).
Axes of the slice: x: 4 (x_hi: 2, x_lo: 2; x = x_hi * 2 + x_lo), y: 4, z: 8, core: 2. Of those that a mesh axis runs over, the one named last changes fastest.
Arguments:
- frames: bfloat16 [2048, 16, 1152], P('clip', 'frame'), may hold values from -6 to 6
- conv_weight: bfloat16 [3, 1152, 1152], replicated, may hold values from -0.109375 to 0.109375
- captions: bfloat16 [2048, 1152], P(('clip', 'frame')), may hold values from -6 to 6
- positive: int32 [2048], P('clip'), may hold values from 0 to 2047, as said below
Outputs:
- loss: float32 [], replicated
- grad_weight: float32 [3, 1152, 1152], P(None, 'clip', 'frame')
- grad_captions: float32 [2048, 1152], P(('clip', 'frame'))
The draws below stay inside these ranges and needn't reach their ends.
Inputs may be any that keep to these rules, and one draw needn't show every extreme that they name: Each caption id is the positive of exactly one clip.
All inputs are finite; a program needn't handle non-finite values.
Results may differ from the reference program's by a relative error of at most 0.0028.
The reference program's roundings to bfloat16 on the way (of `u_low`, `v_low`, `coef` and `dconv`) count: a program that leaves them out, or rounds other values in their place, can miss the bound.
Values may be sent and summed in bfloat16 or wider, within the bound.
No kernel may reach another device: no remote copies, remote signals or barrier semaphores. Data moves between devices by JAX's collectives and lax.ppermute only.
A program may use at most 128 MiB of HBM per device.

```python
import math
import jax
import jax.numpy as jnp
from jax import lax

D = 1152
FRAMES = 16
CLIPS = 2048
CAPTIONS = 2048


def pairing_order(key):
    return jax.random.permutation(jax.random.fold_in(key, 21), CLIPS).astype(jnp.int32)


def caption_base(key, topic_share, common_share):
    order = jax.random.permutation(jax.random.fold_in(key, 11), CAPTIONS).astype(jnp.int32)
    groups = order // 16
    topics = jax.random.normal(jax.random.fold_in(key, 12), (CAPTIONS // 16 + 1, D), jnp.float32)
    noise = jax.random.normal(jax.random.fold_in(key, 13), (CAPTIONS, D), jnp.float32)
    common = jax.random.normal(jax.random.fold_in(key, 14), (1, D), jnp.float32)
    rest = 1.0 - topic_share - common_share
    return math.sqrt(common_share) * common + math.sqrt(topic_share) * topics[groups] + math.sqrt(rest) * noise


def draw_positive(key, part):
    return pairing_order(key)


def draw_captions(key, part):
    topic_share, common_share = (0.7, 0.04)
    base = caption_base(key, topic_share, common_share)
    own = jax.random.fold_in(key, 7)
    scales = jnp.exp(jax.random.uniform(own, (CAPTIONS, 1), jnp.float32, -0.7, 0.7))
    return jnp.clip(base * scales, -6.0, 6.0).astype(jnp.bfloat16)


def draw_frames(key, part):
    topic_share, common_share = (0.7, 0.04)
    base = caption_base(key, topic_share, common_share)
    paired = base[pairing_order(key)]
    own = jax.random.fold_in(key, 3)
    noise = jax.random.normal(own, (CLIPS, FRAMES, D), jnp.float32)
    mixed = 0.8 * paired[:, None, :] + 0.6 * noise
    return jnp.clip(mixed, -6.0, 6.0).astype(jnp.bfloat16)


def centred(key, extent, deviation, bound, held_as=jnp.bfloat16):
    return jnp.clip(deviation * jax.random.normal(key, extent, jnp.float32), -bound, bound).astype(held_as)


def setup_inputs(seed: int = 0) -> dict:
    key_of = jax.random.split(jax.random.key(seed), 5)
    return {
        "frames": draw_frames(jax.random.fold_in(key_of[4], 71), 0),
        "conv_weight": centred(key_of[1], (3, D, D), (3 * D) ** -0.5, 0.109375),
        "captions": draw_captions(jax.random.fold_in(key_of[4], 71), 0),
        "positive": draw_positive(jax.random.fold_in(key_of[4], 71), 0),
    }


def reference(frames, conv_weight, captions, positive):
    clips, nframes, width = frames.shape
    padded = jnp.pad(frames, ((0, 0), (1, 1), (0, 0)))
    shifted = [padded[:, k:k + nframes].reshape(clips * nframes, width) for k in range(3)]
    conv = jnp.dot(shifted[0], conv_weight[0], preferred_element_type=jnp.float32)
    conv = conv + jnp.dot(shifted[1], conv_weight[1], preferred_element_type=jnp.float32)
    conv = conv + jnp.dot(shifted[2], conv_weight[2], preferred_element_type=jnp.float32)
    hidden = frames.reshape(clips * nframes, width).astype(jnp.float32) + jax.nn.gelu(conv)
    pooled = lax.optimization_barrier(jnp.mean(hidden.reshape(clips, nframes, width), axis=1))
    pnorm = jnp.sqrt(lax.optimization_barrier(jnp.sum(pooled * pooled, axis=1, keepdims=True)) + 1e-06)
    unit = pooled / pnorm
    u_low = unit.astype(jnp.bfloat16)
    capf = captions.astype(jnp.float32)
    cnorm = jnp.sqrt(lax.optimization_barrier(jnp.sum(capf * capf, axis=1, keepdims=True)) + 1e-06)
    vunit = capf / cnorm
    v_low = vunit.astype(jnp.bfloat16)
    logits = 10.0 * jnp.dot(u_low, v_low.T, preferred_element_type=jnp.float32) - 10.0
    ids = jnp.arange(captions.shape[0], dtype=jnp.int32)
    match = (positive[:, None] == ids[None, :]).astype(jnp.float32)
    sign = 2.0 * match - 1.0
    loss = jnp.sum(jax.nn.softplus(-sign * logits)) / clips
    coef = (10.0 * (jax.nn.sigmoid(logits) - match)).astype(jnp.bfloat16)
    du = jnp.dot(coef, v_low, preferred_element_type=jnp.float32)
    dv = jnp.dot(coef.T, u_low, preferred_element_type=jnp.float32)
    grad_captions = (dv - vunit * lax.optimization_barrier(jnp.sum(vunit * dv, axis=1, keepdims=True))) / cnorm
    dpooled = (du - unit * lax.optimization_barrier(jnp.sum(unit * du, axis=1, keepdims=True))) / pnorm
    dhidden = jnp.broadcast_to((dpooled / nframes)[:, None, :], (clips, nframes, width)).reshape(clips * nframes, width)
    _, pull = jax.vjp(jax.nn.gelu, conv)
    dconv = pull(dhidden)[0].astype(jnp.bfloat16)
    grads = [lax.dot_general(shifted[k], dconv, (((0,), (0,)), ((), ())), preferred_element_type=jnp.float32) for k in range(3)]
    return (loss, jnp.stack(grads), grad_captions)
```

```python
import jax
import jax.numpy as jnp
import numpy as np
from jax import lax
from jax.sharding import PartitionSpec as P

FRAMES = 16
XH, Y, Z, XL, CORE = 2, 4, 8, 2, 2
BOTH = ("clip", "frame")


def place(index):
    clip, frame = divmod(index, XL * CORE)
    xh, rest = divmod(clip, Y * Z)
    y, z = divmod(rest, Z)
    xl, core = divmod(frame, CORE)
    return xh, y, z, xl, core


def index_of(xh, y, z, xl, core):
    return (((xh * Y + y) * Z + z) * XL + xl) * CORE + core


def swap(value, flip_xh, flip_xl, flip_core):
    pairs = []
    for source in range(XH * Y * Z * XL * CORE):
        xh, y, z, xl, core = place(source)
        pairs.append((source, index_of(xh ^ flip_xh, y, z, xl ^ flip_xl, core ^ flip_core)))
    return lax.ppermute(value, BOTH, pairs)


Z_GROUPS = [[(xh * Y + y) * Z + z for z in range(Z)] for xh in range(XH) for y in range(Y)]
Y_GROUPS = [[(xh * Y + y) * Z + z for y in range(Y)] for xh in range(XH) for z in range(Z)]


def exchange(value, groups):
    return lax.all_to_all(value, "clip", 0, 0, axis_index_groups=groups, tiled=True)


def in_order(parts, pos):
    low, high = pos % 2 == 1, pos // 2 == 1
    parts = [jnp.where(low, parts[j ^ 1], parts[j]) for j in range(4)]
    return [jnp.where(high, parts[j ^ 2], parts[j]) for j in range(4)]


def on_device(frames, conv_weight, captions, positive):
    clip_dev, fr_dev, width = frames.shape
    cap_dev = captions.shape[0]
    clip_pos = lax.axis_index("clip")
    pos = lax.axis_index("frame")
    half, core = clip_pos // (Y * Z), pos % CORE
    cols = width // (XL * CORE)
    group = clip_dev * XH

    capf = captions.astype(jnp.float32)
    cnorm = jnp.sqrt(jnp.sum(capf * capf, axis=1, keepdims=True) + 1e-06)
    vunit = capf / cnorm
    v_low = vunit.astype(jnp.bfloat16)
    piece = exchange(jnp.broadcast_to(v_low, (Z, cap_dev, width)), Z_GROUPS)
    piece = piece.reshape(1, Z * cap_dev, width)
    piece = exchange(jnp.broadcast_to(piece, (Y, Z * cap_dev, width)), Y_GROUPS)
    piece = piece.reshape(Y * Z * cap_dev, width)
    count = piece.shape[0]
    row = jnp.arange(count, dtype=jnp.int32)
    ids = ((half * Y * Z + row // cap_dev) * (XL * CORE) + pos) * cap_dev + row % cap_dev

    mine = jnp.transpose(frames, (1, 0, 2))
    far = [mine, swap(mine, 0, 1, 0), swap(mine, 1, 0, 0), swap(mine, 1, 1, 0)]
    near = [swap(part, 0, 0, 1) for part in far]
    own = in_order([far[0], near[0], far[1], near[1]], pos)
    other = in_order([far[2], near[2], far[3], near[3]], pos)
    zero = jnp.zeros((1, group, width), frames.dtype)
    both = jnp.concatenate(
        [jnp.concatenate(own, axis=0), jnp.concatenate(other, axis=0)], axis=1
    )
    padded = jnp.concatenate([zero, both, zero], axis=0).reshape((FRAMES + 2) * group, width)
    wanted = jnp.concatenate([positive, swap(positive, 1, 0, 0)])

    rows = FRAMES * group
    shifted = [padded[k * group : k * group + rows] for k in range(3)]
    conv = jnp.dot(shifted[0], conv_weight[0], preferred_element_type=jnp.float32)
    conv = conv + jnp.dot(shifted[1], conv_weight[1], preferred_element_type=jnp.float32)
    conv = conv + jnp.dot(shifted[2], conv_weight[2], preferred_element_type=jnp.float32)
    hidden = shifted[1].astype(jnp.float32) + jax.nn.gelu(conv)
    pooled = jnp.sum(hidden.reshape(FRAMES, group, width), axis=0) / FRAMES
    pnorm = jnp.sqrt(jnp.sum(pooled * pooled, axis=1, keepdims=True) + 1e-06)
    unit = pooled / pnorm
    u_low = unit.astype(jnp.bfloat16)

    dots = lax.dot_general(u_low, piece, (((1,), (1,)), ((), ())), preferred_element_type=jnp.float32)
    logits = 10.0 * dots - 10.0
    match = (wanted[:, None] == ids[None, :]).astype(jnp.float32)
    sign = 2.0 * match - 1.0
    total = jnp.sum(jax.nn.softplus(-sign * logits))
    coef = (10.0 * (jax.nn.sigmoid(logits) - match)).astype(jnp.bfloat16)
    du_part = jnp.dot(coef, piece, preferred_element_type=jnp.float32)
    dv_part = lax.dot_general(
        coef, u_low, (((0,), (0,)), ((), ())), preferred_element_type=jnp.float32
    )

    dv = jnp.sum(exchange(dv_part.reshape(Y, Z * cap_dev, width), Y_GROUPS), axis=0)
    dv = jnp.sum(exchange(dv.reshape(Z, cap_dev, width), Z_GROUPS), axis=0)
    grad_captions = (dv - vunit * jnp.sum(vunit * dv, axis=1, keepdims=True)) / cnorm

    along = jnp.sum(unit * du_part, axis=1, keepdims=True)
    tail = jnp.concatenate([along, jnp.broadcast_to(total, (group, 1))], axis=1)
    chunks = [du_part[:, i * cols : (i + 1) * cols] for i in range(4)]
    keep = jnp.concatenate(
        [jnp.where(core == 0, chunks[0], chunks[1]), jnp.where(core == 0, chunks[2], chunks[3]), tail], axis=1
    )
    send = jnp.concatenate(
        [jnp.where(core == 0, chunks[1], chunks[0]), jnp.where(core == 0, chunks[3], chunks[2]), tail], axis=1
    )
    chip = keep + swap(send, 0, 0, 1)
    tail = chip[:, 2 * cols :]
    low, high = chip[:, :cols], chip[:, cols : 2 * cols]
    same = jnp.concatenate([jnp.where(pos // CORE == 0, low, high), tail], axis=1)
    cross = jnp.concatenate([jnp.where(pos // CORE == 0, high, low), tail], axis=1)
    full = same + swap(jnp.roll(same, clip_dev, axis=0), 1, 0, 0)
    full = full + swap(cross, 0, 1, 0) + swap(jnp.roll(cross, clip_dev, axis=0), 1, 1, 0)
    du, along, total = full[:, :cols], full[:, cols : cols + 1], full[0, cols + 1]

    unit_own = lax.dynamic_slice_in_dim(unit, pos * cols, cols, axis=1)
    conv_own = lax.dynamic_slice_in_dim(conv, pos * cols, cols, axis=1)
    dpooled = (du - unit_own * along) / pnorm
    dhidden = jnp.broadcast_to((dpooled / FRAMES)[None], (FRAMES, group, cols)).reshape(rows, cols)
    _, pull = jax.vjp(jax.nn.gelu, conv_own)
    dconv = pull(dhidden)[0].astype(jnp.bfloat16)
    part_rows = width // XH
    left = lax.dynamic_slice_in_dim(padded, half * part_rows, part_rows, axis=1)
    terms = [
        lax.dot_general(
            left[k * group : k * group + rows], dconv, (((0,), (0,)), ((), ())), preferred_element_type=jnp.float32
        )
        for k in range(3)
    ]
    first = lax.reduce_precision(total, 8, 7)
    second = lax.reduce_precision(total - first, 8, 7)
    third = lax.reduce_precision(total - first - second, 8, 7)
    spare = -(-3 * cols // 128) * 128 - 3 * cols
    if spare < 3:
        spare += 128
    extra = jnp.concatenate([jnp.stack([first, second, third]), jnp.zeros((spare - 3,), jnp.float32)])
    terms = jnp.concatenate(terms + [jnp.broadcast_to(extra, (part_rows, spare))], axis=1)
    out = exchange(terms.astype(jnp.bfloat16).reshape(Y, part_rows // Y, 3 * cols + spare), Y_GROUPS)
    out = jnp.sum(out.astype(jnp.float32), axis=0)
    out = exchange(out.reshape(Z, part_rows // (Y * Z), 3 * cols + spare), Z_GROUPS)
    out = jnp.sum(out, axis=0)
    loss = jnp.sum(out[0, 3 * cols : 3 * cols + 3]) / (clip_dev * lax.axis_size("clip"))
    grad_weight = jnp.stack([out[:, k * cols : (k + 1) * cols] for k in range(3)])
    return (loss, grad_weight, grad_captions)


def solution(mesh):
    placed = (P("clip", "frame", None), P(), P(("clip", "frame"), None), P("clip"))
    return jax.shard_map(
        on_device,
        mesh=mesh,
        in_specs=placed,
        out_specs=(P(), P(None, "clip", "frame"), P(("clip", "frame"), None)),
        check_vma=False,
    )
```

```python
import functools
import math

import jax
import jax.numpy as jnp
from jax import lax
from jax.experimental import pallas as pl
from jax.experimental.pallas import tpu as pltpu
from jax.sharding import PartitionSpec as P

FRAMES = 16
XH, Y, Z, XL, CORE = 2, 4, 8, 2, 2
BOTH = ("clip", "frame")
F32, BF16 = jnp.float32, jnp.bfloat16
ROOT = math.sqrt(2.0 / math.pi)
CUBE = 0.044715


def place(index):
    clip, frame = divmod(index, XL * CORE)
    xh, rest = divmod(clip, Y * Z)
    y, z = divmod(rest, Z)
    xl, core = divmod(frame, CORE)
    return xh, y, z, xl, core


def index_of(xh, y, z, xl, core):
    return (((xh * Y + y) * Z + z) * XL + xl) * CORE + core


def swap(value, flip_xh, flip_xl, flip_core):
    pairs = []
    for source in range(XH * Y * Z * XL * CORE):
        xh, y, z, xl, core = place(source)
        pairs.append((source, index_of(xh ^ flip_xh, y, z, xl ^ flip_xl, core ^ flip_core)))
    return lax.ppermute(value, BOTH, pairs)


def move(value, by_y, by_z):
    pairs = []
    for source in range(XH * Y * Z * XL * CORE):
        xh, y, z, xl, core = place(source)
        pairs.append((source, index_of(xh, (y + by_y) % Y, (z + by_z) % Z, xl, core)))
    return lax.ppermute(value, BOTH, pairs)


Z_GROUPS = [[(xh * Y + y) * Z + z for z in range(Z)] for xh in range(XH) for y in range(Y)]
YZ_GROUPS = [[xh * Y * Z + yz for yz in range(Y * Z)] for xh in range(XH)]


def exchange(value, groups):
    return lax.all_to_all(value, "clip", 0, 0, axis_index_groups=groups, tiled=True)


def roundup(value, unit):
    return -(-value // unit) * unit


def whereabouts():
    clip = lax.axis_index("clip")
    return lax.axis_index("frame"), clip // (Y * Z), clip // Z % Y, clip % Z


def call(body, mib, out_shapes, scratch, flops, moved, *operands, loose={}, far={}):
    specs = []
    operands = list(operands)
    for i, o in enumerate(operands):
        space = loose.get(i, pltpu.VMEM)
        if space is pltpu.HBM:
            operands[i] = pltpu.with_memory_space_constraint(o, space)
        specs.append(pl.BlockSpec(memory_space=space))
    return pl.pallas_call(
        body,
        out_shape=[
            far[i](s, d) if i in far else jax.ShapeDtypeStruct(s, d) for i, (s, d) in enumerate(out_shapes)
        ],
        in_specs=specs,
        out_specs=[pl.BlockSpec(memory_space=far.get(i, pltpu.VMEM)) for i in range(len(out_shapes))],
        scratch_shapes=scratch,
        cost_estimate=pl.CostEstimate(flops=flops, bytes_accessed=moved, transcendentals=0),
        compiler_params=pltpu.CompilerParams(vmem_limit_bytes=mib * 2**20),
    )(*operands)


def conv_kernel(cols, *refs):
    pieces, weights, (x_ref, out_ref, pooled_ref, slope_ref, w_ref, sum_ref, part_ref, x_sem, w_sem, o_sem) = (
        refs[:8],
        refs[8],
        refs[9:],
    )
    frame, half, _, _ = whereabouts()
    steps, block, width = pieces[0].shape
    group = pooled_ref.shape[0]
    wide = slope_ref.shape[2]
    copies = []
    for i, piece in enumerate(pieces):
        j, side = i % 4, i // 4
        first = (frame ^ j) * steps + 1
        start = pl.multiple_of((half ^ side) * block, block)
        copies.append(
            pltpu.make_async_copy(
                piece, x_ref.at[pl.ds(first, steps), pl.ds(start, block), :], x_sem.at[i]
            )
        )
    for k in range(3):
        for i in range(XL):
            start = pl.multiple_of((frame ^ (i * CORE)) * (wide - 128), 128)
            copies.append(
                pltpu.make_async_copy(
                    weights.at[k, :, pl.ds(start, wide)], w_ref.at[k, :, pl.ds(i * wide, wide)], w_sem.at[k, i]
                )
            )
    for copy in copies:
        copy.start()
    filled = copies[len(pieces) :]
    x_ref[0] = jnp.zeros((group, width), BF16)
    x_ref[FRAMES + 1] = jnp.zeros((group, width), BF16)
    sum_ref[...] = jnp.zeros_like(sum_ref)
    part_ref[...] = jnp.zeros_like(part_ref)
    for copy in copies[: len(pieces)]:
        copy.wait()

    def step(m, first):
        base = m * steps
        conv = jnp.zeros((steps * group, XL * wide), F32)
        for k in range(3):
            if first:
                for copy in filled[k * XL : (k + 1) * XL]:
                    copy.wait()
            rows = x_ref[pl.ds(base + k, steps)].reshape(steps * group, width)
            conv = conv + jnp.dot(rows, w_ref[k], preferred_element_type=F32)
        tanh = jnp.tanh(ROOT * conv * (1.0 + CUBE * (conv * conv)))
        gelu = 0.5 * conv * (1.0 + tanh)
        part_ref[...] += jnp.sum(gelu.reshape(steps, group, XL * wide), axis=0)
        conv, tanh = conv[:, :wide], tanh[:, :wide]
        slope = 0.5 * (1.0 + tanh) + 0.5 * conv * (1.0 - tanh * tanh) * (
            ROOT * (1.0 + 3.0 * CUBE * (conv * conv))
        )
        slope_ref[pl.ds(base, steps)] = slope.reshape(steps, group, wide)
        sum_ref[...] += jnp.sum(x_ref[pl.ds(base + 1, steps)].astype(F32), axis=0)

    stores = []
    for m in range(FRAMES // steps):
        step(m, m == 0)
        rows = pl.ds(m * steps, steps)
        stores.append(pltpu.make_async_copy(slope_ref.at[rows], out_ref.at[rows], o_sem.at[m]))
        stores[-1].start()
    shift = cols + 128 - wide
    for f in range(XL * CORE):

        @pl.when(frame == f)
        def _():
            for i in range(XL):
                g = f ^ (i * CORE)
                gelu = part_ref[:, i * wide + g * shift : i * wide + g * shift + cols]
                pooled_ref[:, i * cols : (i + 1) * cols] = (
                    sum_ref[:, g * cols : (g + 1) * cols] + gelu
                ) / FRAMES

    for store in stores:
        store.wait()


def pair_kernel(cap_dev, mine, peer, v_ref, positive, across, *refs):
    (keep_ref, send_ref, unit_ref, norm_ref), dv_refs, (pooled_ref, lay_ref) = refs[:4], refs[4 : 4 + Y], refs[4 + Y :]
    frame, half, y_pos, _ = whereabouts()
    part = mine.shape[1]
    cols = part // 2
    group = mine.shape[0]
    pooled_ref[:, 0:part] = mine[...]
    pooled_ref[:, part : 2 * part] = peer[...]
    pooled = pooled_ref[...]
    pnorm = jnp.sqrt(jnp.sum(pooled * pooled, axis=1, keepdims=True) + 1e-06)
    unit = pooled / pnorm
    u_low = unit.astype(BF16)
    v_low = v_ref[...]
    dots = lax.dot_general(u_low, v_low, (((1,), (1,)), ((), ())), preferred_element_type=F32)
    logits = 10.0 * dots - 10.0
    first = jnp.where(half == 0, positive[...], across[...])
    second = jnp.where(half == 0, across[...], positive[...])
    wanted = jnp.concatenate([first, second], axis=0)
    row = lax.broadcasted_iota(jnp.int32, (1, v_low.shape[0]), 1)
    ids = ((half * (Y * Z) + row // cap_dev) * (XL * CORE) + frame) * cap_dev + row % cap_dev
    match = jnp.where(wanted == ids, 1.0, 0.0).astype(F32)
    sign = 2.0 * match - 1.0
    turned = -sign * logits
    terms = jnp.maximum(turned, 0.0) + jnp.log1p(jnp.exp(-jnp.abs(turned)))
    total = jnp.sum(jnp.sum(terms, axis=1, keepdims=True), axis=0, keepdims=True)
    coef = (10.0 * (1.0 / (1.0 + jnp.exp(-logits)) - match)).astype(BF16)
    du = jnp.dot(coef, v_low, preferred_element_type=F32)
    dv = lax.dot_general(coef, u_low, (((0,), (0,)), ((), ())), preferred_element_type=F32)
    lay_ref[...] = dv.reshape(lay_ref.shape)
    for i, dv_ref in enumerate(dv_refs):
        dv_ref[...] = lay_ref[(y_pos + i) % Y]
    along = jnp.sum(unit * du, axis=1, keepdims=True)
    pooled_ref[...] = du
    spare = keep_ref.shape[1] - part
    lane = lax.broadcasted_iota(jnp.int32, (group, spare), 1)
    tail = jnp.where(lane == 0, along, jnp.where(lane == 1, total, 0.0))
    keep_ref[:, 0:part] = pooled_ref[:, 0:part]
    send_ref[:, 0:part] = pooled_ref[:, part : 2 * part]
    keep_ref[:, part:] = tail
    send_ref[:, part:] = tail
    unit_ref[...] = unit[:, 0:cols]
    norm_ref[...] = pnorm


def weight_kernel(s0, s1, s2, s3, unit, norm, slope_in, x_ref, *refs):
    outs, (d_ref, g_ref, p_ref, c_ref, slope, sem) = refs[:Y], refs[Y:]
    load = pltpu.make_async_copy(slope_in, slope, sem)
    load.start()
    frame, half, y_pos, _ = whereabouts()
    group, cols = unit.shape
    width = x_ref.shape[2]
    wide = slope.shape[2]
    shift = cols + 128 - wide
    share = outs[0].shape[0]
    full = s0[...] + s1[...] + s2[...] + s3[...]
    along, total = full[:, cols : cols + 1], full[0:1, cols + 1 : cols + 2]
    dpooled = (full[:, 0:cols] - unit[...] * along) / norm[...] / FRAMES
    p_ref[...] = jnp.zeros_like(p_ref)
    for f in range(XL * CORE):

        @pl.when(frame == f)
        def _():
            p_ref[:, f * shift : f * shift + cols] = dpooled

    dpooled = p_ref[...]
    zero = jnp.zeros((group, wide), BF16)
    for k in range(3):
        for t in range(FRAMES + 2):
            if t < k or t >= FRAMES + k:
                d_ref[t * group : (t + 1) * group, k * wide : (k + 1) * wide] = zero
    load.wait()
    for t in range(FRAMES):
        dconv = (slope[t] * dpooled).astype(BF16)
        for k in range(3):
            d_ref[(t + k) * group : (t + k + 1) * group, k * wide : (k + 1) * wide] = dconv
    tile = 128
    tiles = roundup(Y * share, tile) // tile
    offset = width - tiles * tile

    def step(m, carry):
        start = pl.multiple_of(half * offset + m * tile, tile)
        rows = x_ref[:, :, pl.ds(start, tile)].reshape((FRAMES + 2) * group, tile)
        g_ref[pl.ds(pl.multiple_of(m * tile, tile), tile), :] = lax.dot_general(
            rows, d_ref[...], (((0,), (0,)), ((), ())), preferred_element_type=F32
        )
        return carry

    lax.fori_loop(0, tiles, step, 0)
    skip = tiles * tile - Y * share
    lane = lax.broadcasted_iota(jnp.int32, (share, c_ref.shape[1] - 3 * cols), 1)
    c_ref[:, 3 * cols :] = loss_lanes(total, lane)
    for i, out_ref in enumerate(outs):
        start = pl.multiple_of(half * skip + ((y_pos + i) % Y) * share, 16)
        for f in range(XL * CORE):

            @pl.when(frame == f)
            def _():
                for k in range(3):
                    c_ref[:, k * cols : (k + 1) * cols] = g_ref[
                        pl.ds(start, share), k * wide + f * shift : k * wide + f * shift + cols
                    ]

        out_ref[...] = c_ref[...].astype(BF16)


def loss_lanes(total, lane):
    first = total.astype(BF16).astype(F32)
    second = (total - first).astype(BF16).astype(F32)
    third = total - first - second
    return jnp.where(lane == 0, first, jnp.where(lane == 1, second, jnp.where(lane == 2, third, 0.0)))


def along_y_kernel(first_lane, *refs):
    ins, caps, (out_ref, sum_ref, lay_ref) = refs[:Y], refs[Y : 2 * Y], refs[2 * Y :]
    rows, lanes = ins[0].shape[0] // Z, ins[0].shape[1]
    kept, packed = lay_ref.shape[1:]
    total = ins[0][...].astype(F32)
    for part in ins[1:]:
        total = total + part[...].astype(F32)
    sum_ref[...] = total
    loss = jnp.sum(sum_ref[0:1, first_lane : first_lane + 3], axis=1, keepdims=True)
    lane = lax.broadcasted_iota(jnp.int32, (1, lanes - first_lane), 1)
    tail = loss_lanes(loss, lane)
    lay_ref[...] = jnp.zeros_like(lay_ref)
    for z in range(Z):
        sum_ref[z * rows : z * rows + 1, first_lane:] = tail
        lay_ref[z, :, 0:lanes] = sum_ref[z * rows : z * rows + kept, :]
        for j in range(rows - kept):
            for i in range(lanes // 128):
                at = j * (lanes // 128) + i
                lay_ref[z, at : at + 1, lanes:] = sum_ref[
                    z * rows + kept + j : z * rows + kept + j + 1, i * 128 : (i + 1) * 128
                ]
    out_ref[:, :, 0:packed] = lay_ref[...].astype(BF16)
    total = caps[0][...]
    for part in caps[1:]:
        total = total + part[...]
    high = total.astype(BF16).astype(F32)
    low = total - high
    own = total.shape[0] // Z
    for z in range(Z):
        both = jnp.concatenate([high[z * own : (z + 1) * own], low[z * own : (z + 1) * own]], axis=0)
        out_ref[z, :, packed:] = both.astype(BF16)


def along_z_kernel(lanes, packed, in_ref, captions, grad_ref, loss_ref, cap_ref, sum_ref, turn_ref):
    rows, cols = grad_ref.shape[1:]
    kept = in_ref.shape[1]
    own, width = captions.shape
    total = in_ref[0].astype(F32)
    for z in range(1, Z):
        total = total + in_ref[z].astype(F32)
    sum_ref[0:kept, :] = total
    for j in range(rows - kept):
        for i in range(lanes // 128):
            at = j * (lanes // 128) + i
            sum_ref[kept + j : kept + j + 1, i * 128 : (i + 1) * 128] = sum_ref[at : at + 1, lanes:packed]
    for k in range(3):
        grad_ref[k] = sum_ref[0:rows, k * cols : (k + 1) * cols]
    loss_ref[...] = jnp.sum(sum_ref[0:1, 3 * cols : 3 * cols + 3], axis=1, keepdims=True)
    frame = whereabouts()[0]
    for f in range(len(ORDER)):

        @pl.when(frame == f)
        def _():
            for i, j in enumerate(ORDER):
                g = f ^ j
                at = packed + i * cols
                turn_ref[:, g * cols : (g + 1) * cols] = (
                    sum_ref[0:own, at : at + cols] + sum_ref[own : 2 * own, at : at + cols]
                )

    dv = turn_ref[...]
    cnorm, unit = norm_of(captions[...])
    cap_ref[...] = (dv - unit * jnp.sum(unit * dv, axis=1, keepdims=True)) / cnorm


ORDER = (0, CORE, 1, CORE ^ 1)


def norm_of(captions):
    capf = captions.astype(F32)
    cnorm = jnp.sqrt(jnp.sum(capf * capf, axis=1, keepdims=True) + 1e-06)
    return cnorm, capf / cnorm


def caption_kernel(captions, out_ref, unit_ref, turn_ref):
    frame = whereabouts()[0]
    cols = captions.shape[1] // len(ORDER)
    unit_ref[...] = norm_of(captions[...])[1]
    for f in range(len(ORDER)):

        @pl.when(frame == f)
        def _():
            for i, j in enumerate(ORDER):
                g = f ^ j
                turn_ref[:, i * cols : (i + 1) * cols] = unit_ref[:, g * cols : (g + 1) * cols]

    low = turn_ref[...].astype(BF16)
    out_ref[...] = jnp.broadcast_to(low[None], out_ref.shape)


def on_device(frames, conv_weight, captions, positive):
    clip_dev, fr_dev, width = frames.shape
    cap_dev = captions.shape[0]
    cols = width // (XL * CORE)
    group = clip_dev * XH
    rows = FRAMES * group

    mine = jnp.transpose(frames, (1, 0, 2))
    first = swap(mine, 0, 0, 1)
    far = [swap(mine, 0, 1, 0), swap(mine, 1, 0, 0), swap(mine, 1, 1, 0)]
    positive = positive[:, None]
    across = swap(positive, 1, 0, 0)
    far[1], across = lax.optimization_barrier((far[1], across))
    near = [first] + [swap(part, 0, 0, 1) for part in far]
    far = [mine] + far
    given = captions
    pieces = [far[0], near[0], far[1], near[1], far[2], near[2], far[3], near[3]]

    (spread,) = call(
        caption_kernel,
        4,
        [((Y * Z, cap_dev, width), BF16)],
        [pltpu.VMEM((cap_dev, width), F32), pltpu.VMEM((cap_dev, width), F32)],
        0,
        Y * Z * cap_dev * width * 2,
        given,
    )
    piece = exchange(spread, YZ_GROUPS).reshape(Y * Z * cap_dev, width)
    count = piece.shape[0]
    wide = cols + (XL * CORE - 1) * (cols % 128)
    x, slope, pooled = call(
        functools.partial(conv_kernel, cols),
        24,
        [((FRAMES + 2, group, width), BF16), ((FRAMES, group, wide), F32), ((group, XL * cols), F32)],
        [
            pltpu.VMEM((FRAMES, group, wide), F32),
            pltpu.VMEM((3, width, XL * wide), BF16),
            pltpu.VMEM((group, width), F32),
            pltpu.VMEM((group, XL * wide), F32),
            pltpu.SemaphoreType.DMA((8,)),
            pltpu.SemaphoreType.DMA((3, XL)),
            pltpu.SemaphoreType.DMA((FRAMES // fr_dev,)),
        ],
        int(3 * rows * 3 * width * 2 * cols),
        3 * width * 2 * wide * 2,
        *pieces,
        conv_weight,
        loose={i: pl.ANY for i in range(8)} | {8: pltpu.HBM},
        far={1: pltpu.HBM},
    )
    pooled, piece = lax.optimization_barrier((pooled, piece))
    peer = swap(pooled, 0, 0, 1)
    lanes = roundup(2 * cols + 2, 128)
    keep, send, unit, pnorm, *dv = call(
        functools.partial(pair_kernel, cap_dev),
        8,
        [((group, lanes), F32), ((group, lanes), F32), ((group, cols), F32), ((group, 1), F32)]
        + [((count // Y, width), F32)] * Y,
        [pltpu.VMEM((group, width), F32), pltpu.VMEM((Y, count // Y, width), F32)],
        6 * group * count * width,
        count * width * 6,
        pooled,
        peer,
        piece,
        positive,
        across,
    )

    chip = keep + swap(send, 0, 0, 1)
    chip, *dv = lax.optimization_barrier((chip, *dv))
    tail = chip[:, 2 * cols : 2 * cols + 2]
    spare = jnp.zeros((group, roundup(cols + 2, 128) - cols - 2), F32)
    same = jnp.concatenate([chip[:, :cols], tail, spare], axis=1)
    cross = jnp.concatenate([chip[:, cols : 2 * cols], tail, spare], axis=1)
    parts = [same, swap(same, 1, 0, 0), swap(cross, 0, 1, 0), swap(cross, 1, 1, 0)]

    share = width // XH // Y
    packed = roundup(3 * cols + 3, 128)
    terms = call(
        weight_kernel,
        16,
        [((share, packed), BF16)] * Y,
        [
            pltpu.VMEM((rows + 2 * group, 3 * wide), BF16),
            pltpu.VMEM((roundup(Y * share, 128), 3 * wide), F32),
            pltpu.VMEM((group, wide), F32),
            pltpu.VMEM((share, packed), F32),
            pltpu.VMEM((FRAMES, group, wide), F32),
            pltpu.SemaphoreType.DMA(()),
        ],
        6 * rows * Y * share * cols,
        rows * width * 2,
        *parts,
        unit,
        pnorm,
        slope,
        x,
        loose={6: pltpu.HBM},
    )
    dv = [dv[0]] + [move(dv[i], i, 0) for i in range(1, Y)]
    terms = [terms[0]] + [move(terms[i], i, 0) for i in range(1, Y)]
    own_rows = share // Z
    kept = own_rows // 16 * 16
    (terms,) = call(
        functools.partial(along_y_kernel, 3 * cols),
        8,
        [((Z, kept, packed + 128 + width), BF16)],
        [pltpu.VMEM((share, packed), F32), pltpu.VMEM((Z, kept, packed + 128), F32)],
        0,
        share * packed * 16,
        *terms,
        *dv,
    )
    terms = exchange(terms, Z_GROUPS)
    grad_weight, loss, grad_captions = call(
        functools.partial(along_z_kernel, packed, packed + 128),
        4,
        [((3, own_rows, cols), F32), ((1, 1), F32), ((cap_dev, width), F32)],
        [pltpu.VMEM((roundup(own_rows, 8), packed + 128 + width), F32), pltpu.VMEM((cap_dev, width), F32)],
        0,
        share * packed * 2,
        terms,
        captions,
    )
    loss = loss[0, 0] / (clip_dev * lax.axis_size("clip"))
    return (loss, grad_weight, grad_captions)


def solution(mesh):
    placed = (P("clip", "frame", None), P(), P(("clip", "frame"), None), P("clip"))
    return jax.shard_map(
        on_device,
        mesh=mesh,
        in_specs=placed,
        out_specs=(P(), P(None, "clip", "frame"), P(("clip", "frame"), None)),
        check_vma=False,
    )
```

```python
import functools
import math

import jax
import jax.numpy as jnp
from jax import lax
from jax.experimental import pallas as pl
from jax.experimental.pallas import tpu as pltpu
from jax.sharding import PartitionSpec as P

FRAMES = 16
XH, Y, Z, XL, CORE = 2, 4, 8, 2, 2
BOTH = ("clip", "frame")
F32, BF16 = jnp.float32, jnp.bfloat16
ROOT = math.sqrt(2.0 / math.pi)
CUBE = 0.044715


def place(index):
    clip, frame = divmod(index, XL * CORE)
    xh, rest = divmod(clip, Y * Z)
    y, z = divmod(rest, Z)
    xl, core = divmod(frame, CORE)
    return xh, y, z, xl, core


def index_of(xh, y, z, xl, core):
    return (((xh * Y + y) * Z + z) * XL + xl) * CORE + core


def swap(value, flip_xh, flip_xl, flip_core):
    pairs = []
    for source in range(XH * Y * Z * XL * CORE):
        xh, y, z, xl, core = place(source)
        pairs.append((source, index_of(xh ^ flip_xh, y, z, xl ^ flip_xl, core ^ flip_core)))
    return lax.ppermute(value, BOTH, pairs)


def move(value, by_y, by_z):
    pairs = []
    for source in range(XH * Y * Z * XL * CORE):
        xh, y, z, xl, core = place(source)
        pairs.append((source, index_of(xh, (y + by_y) % Y, (z + by_z) % Z, xl, core)))
    return lax.ppermute(value, BOTH, pairs)


Z_GROUPS = [[(xh * Y + y) * Z + z for z in range(Z)] for xh in range(XH) for y in range(Y)]
YZ_GROUPS = [[xh * Y * Z + yz for yz in range(Y * Z)] for xh in range(XH)]


def exchange(value, groups):
    return lax.all_to_all(value, "clip", 0, 0, axis_index_groups=groups, tiled=True)


def roundup(value, unit):
    return -(-value // unit) * unit


def whereabouts():
    clip = lax.axis_index("clip")
    return lax.axis_index("frame"), clip // (Y * Z), clip // Z % Y, clip % Z


def call(body, mib, out_shapes, scratch, flops, moved, *operands, loose={}, far={}):
    specs = []
    operands = list(operands)
    for i, o in enumerate(operands):
        space = loose.get(i, pltpu.VMEM)
        if space is pltpu.HBM:
            operands[i] = pltpu.with_memory_space_constraint(o, space)
        specs.append(pl.BlockSpec(memory_space=space))
    return pl.pallas_call(
        body,
        out_shape=[
            far[i](s, d) if i in far else jax.ShapeDtypeStruct(s, d) for i, (s, d) in enumerate(out_shapes)
        ],
        in_specs=specs,
        out_specs=[pl.BlockSpec(memory_space=far.get(i, pltpu.VMEM)) for i in range(len(out_shapes))],
        scratch_shapes=scratch,
        cost_estimate=pl.CostEstimate(flops=flops, bytes_accessed=moved, transcendentals=0),
        compiler_params=pltpu.CompilerParams(vmem_limit_bytes=mib * 2**20),
    )(*operands)


def conv_kernel(cols, *refs):
    (mine, *near, held), w_ref, (x_ref, out_ref, mean_ref, slope_ref, sum_ref, part_ref, pooled_ref, x_sem, o_sem) = (
        refs[:6],
        refs[6],
        refs[7:],
    )
    far = [mine] + [held.at[i] for i in range(held.shape[0])]
    pieces = [far[0], near[0], far[1], near[1], far[2], near[2], far[3], near[3]]
    frame, half, _, _ = whereabouts()
    steps, block, width = mine.shape
    group = pooled_ref.shape[0]
    wide = slope_ref.shape[2]
    copies = []
    for i, piece in enumerate(pieces):
        j, side = i % 4, i // 4
        first = (frame ^ j) * steps + 1
        start = pl.multiple_of((half ^ side) * block, block)
        copies.append(
            pltpu.make_async_copy(
                piece, x_ref.at[pl.ds(first, steps), pl.ds(start, block), :], x_sem.at[i]
            )
        )
    for copy in copies:
        copy.start()
    x_ref[0] = jnp.zeros((group, width), BF16)
    x_ref[FRAMES + 1] = jnp.zeros((group, width), BF16)
    sum_ref[...] = jnp.zeros_like(sum_ref)
    part_ref[...] = jnp.zeros_like(part_ref)
    for copy in copies:
        copy.wait()

    def step(m):
        base = m * steps
        conv = None
        for k in range(3):
            rows = x_ref[pl.ds(base + k, steps)].reshape(steps * group, width)
            term = jnp.dot(rows, w_ref[k], preferred_element_type=F32)
            conv = term if conv is None else conv + term
        tanh = jnp.tanh(conv * (ROOT + (ROOT * CUBE) * (conv * conv)))
        part = 0.5 * conv
        gelu = part + part * tanh
        part_ref[...] += jnp.sum(gelu.reshape(steps, group, XL * wide), axis=0)
        conv, tanh, part = conv[:, :wide], tanh[:, :wide], part[:, :wide]
        slope = 0.5 * (1.0 + tanh) + part * (1.0 - tanh * tanh) * (
            ROOT + (3.0 * ROOT * CUBE) * (conv * conv)
        )
        slope_ref[pl.ds(base, steps)] = slope.reshape(steps, group, wide)
        sum_ref[...] += jnp.sum(x_ref[pl.ds(base + 1, steps)].astype(F32), axis=0)

    stores = []
    for m in range(FRAMES // steps):
        step(m)
        rows = pl.ds(m * steps, steps)
        stores.append(pltpu.make_async_copy(slope_ref.at[rows], out_ref.at[rows], o_sem.at[m]))
        stores[-1].start()
    shift = cols + 128 - wide
    for f in range(XL * CORE):

        @pl.when(frame == f)
        def _():
            for i in range(XL):
                g = f ^ (i * CORE)
                gelu = part_ref[:, i * wide + g * shift : i * wide + g * shift + cols]
                pooled_ref[:, i * cols : (i + 1) * cols] = (
                    sum_ref[:, g * cols : (g + 1) * cols] + gelu
                ) / FRAMES

    stores.append(pltpu.make_async_copy(pooled_ref, mean_ref, o_sem.at[FRAMES // steps]))
    stores[-1].start()
    for store in stores:
        store.wait()


def pair_kernel(cap_dev, pooled_in, peer, v_ref, wanted, *refs):
    (keep_ref, send_ref, unit_ref, norm_ref), dv_refs, (pooled_ref, lay_ref, mine, near_ref, sem) = refs[:4], refs[4 : 4 + Y], refs[4 + Y :]
    first = pltpu.make_async_copy(pooled_in, mine, sem.at[0])
    first.start()
    load = pltpu.make_async_copy(wanted, near_ref, sem.at[1])
    load.start()
    first.wait()
    frame, half, y_pos, _ = whereabouts()
    part = mine.shape[1]
    cols = part // 2
    group = mine.shape[0]
    pooled_ref[:, 0:part] = mine[...]
    pooled_ref[:, part : 2 * part] = peer[...]
    pooled = pooled_ref[...]
    pnorm = jnp.sqrt(jnp.sum(pooled * pooled, axis=1, keepdims=True) + 1e-06)
    unit = pooled / pnorm
    u_low = unit.astype(BF16)
    v_low = v_ref[...]
    dots = lax.dot_general(u_low, v_low, (((1,), (1,)), ((), ())), preferred_element_type=F32)
    logits = 10.0 * dots - 10.0
    row = lax.broadcasted_iota(jnp.int32, (1, v_low.shape[0]), 1)
    ids = ((half * (Y * Z) + row // cap_dev) * (XL * CORE) + frame) * cap_dev + row % cap_dev
    load.wait()
    match = jnp.where(near_ref[...] == ids, 1.0, 0.0).astype(F32)
    sign = 2.0 * match - 1.0
    turned = -sign * logits
    terms = jnp.maximum(turned, 0.0) + jnp.log1p(jnp.exp(-jnp.abs(turned)))
    total = jnp.sum(jnp.sum(terms, axis=1, keepdims=True), axis=0, keepdims=True)
    grad = 10.0 * (1.0 / (1.0 + jnp.exp(-logits)) - match)
    coef = grad.astype(BF16)
    du = jnp.dot(coef, v_low, preferred_element_type=F32)
    share = coef.shape[1] // Y
    for y in range(Y):
        block = grad[:, y * share : (y + 1) * share]
        pad = jnp.zeros((group, lay_ref.shape[2] - share), F32)
        lay_ref[y] = jnp.concatenate([block, pad], axis=1).astype(BF16)
    for i, dv_ref in enumerate(dv_refs):
        dv_ref[:, 0 : 2 * part] = u_low
        dv_ref[:, 2 * part :] = lay_ref[(y_pos + i) % Y]
    along = jnp.sum(unit * du, axis=1, keepdims=True)
    pooled_ref[...] = du
    spare = keep_ref.shape[1] - part
    lane = lax.broadcasted_iota(jnp.int32, (group, spare), 1)
    tail = jnp.where(lane == 0, along, jnp.where(lane == 1, total, 0.0))
    keep_ref[:, 0:part] = pooled_ref[:, 0:part]
    send_ref[:, 0:part] = pooled_ref[:, part : 2 * part]
    keep_ref[:, part:] = tail
    send_ref[:, part:] = tail
    unit_ref[...] = unit[:, 0:cols]
    norm_ref[...] = pnorm


def turn_kernel(x_ref, out_ref):
    half = whereabouts()[1]
    tile = 128
    tiles = out_ref.shape[0] // tile
    offset = x_ref.shape[2] - tiles * tile
    for m in range(tiles):
        start = pl.multiple_of(half * offset + m * tile, tile)
        rows = x_ref[:, :, pl.ds(start, tile)].reshape(x_ref.shape[0] * x_ref.shape[1], tile)
        out_ref[m * tile : (m + 1) * tile, :] = rows.T


def weight_kernel(s0, s1, s2, s3, unit, norm, slope_in, x_ref, *refs):
    outs, (d_ref, g_ref, p_ref, c_ref, slope, sem) = refs[:Y], refs[Y:]
    load = pltpu.make_async_copy(slope_in, slope, sem)
    load.start()
    frame, half, y_pos, _ = whereabouts()
    group, cols = unit.shape
    wide = slope.shape[2]
    shift = cols + 128 - wide
    share = outs[0].shape[0]
    full = s0[...] + s1[...] + s2[...] + s3[...]
    along, total = full[:, cols : cols + 1], full[0:1, cols + 1 : cols + 2]
    dpooled = (full[:, 0:cols] - unit[...] * along) / norm[...] / FRAMES
    p_ref[...] = jnp.zeros_like(p_ref)
    for f in range(XL * CORE):

        @pl.when(frame == f)
        def _():
            p_ref[:, f * shift : f * shift + cols] = dpooled

    dpooled = p_ref[...]
    zero = jnp.zeros((group, wide), BF16)
    for k in range(3):
        for t in range(FRAMES + 2):
            if t < k or t >= FRAMES + k:
                d_ref[t * group : (t + 1) * group, k * wide : (k + 1) * wide] = zero
    load.wait()
    for t in range(FRAMES):
        dconv = (slope[t] * dpooled).astype(BF16)
        for k in range(3):
            d_ref[(t + k) * group : (t + k + 1) * group, k * wide : (k + 1) * wide] = dconv
    g_ref[...] = jnp.dot(x_ref[...], d_ref[...], preferred_element_type=F32)
    skip = x_ref.shape[0] - Y * share
    lane = lax.broadcasted_iota(jnp.int32, (share, c_ref.shape[1] - 3 * cols), 1)
    c_ref[:, 3 * cols :] = loss_lanes(total, lane)
    for i, out_ref in enumerate(outs):
        start = pl.multiple_of(half * skip + ((y_pos + i) % Y) * share, 16)
        for f in range(XL * CORE):

            @pl.when(frame == f)
            def _():
                for k in range(3):
                    c_ref[:, k * cols : (k + 1) * cols] = g_ref[
                        pl.ds(start, share), k * wide + f * shift : k * wide + f * shift + cols
                    ]

        out_ref[...] = c_ref[...].astype(BF16)


def loss_lanes(total, lane):
    first = total.astype(BF16).astype(F32)
    second = (total - first).astype(BF16).astype(F32)
    third = total - first - second
    return jnp.where(lane == 0, first, jnp.where(lane == 1, second, jnp.where(lane == 2, third, 0.0)))


def along_y_kernel(first_lane, *refs):
    ins, caps, (out_ref, sum_ref, lay_ref) = refs[:Y], refs[Y], refs[Y + 1 :]
    rows, lanes = ins[0].shape[0] // Z, ins[0].shape[1]
    kept, packed = lay_ref.shape[1:]
    total = ins[0][...].astype(F32)
    for part in ins[1:]:
        total = total + part[...].astype(F32)
    sum_ref[...] = total
    loss = jnp.sum(sum_ref[0:1, first_lane : first_lane + 3], axis=1, keepdims=True)
    lane = lax.broadcasted_iota(jnp.int32, (1, lanes - first_lane), 1)
    tail = loss_lanes(loss, lane)
    lay_ref[...] = jnp.zeros_like(lay_ref)
    for z in range(Z):
        sum_ref[z * rows : z * rows + 1, first_lane:] = tail
        lay_ref[z, :, 0:lanes] = sum_ref[z * rows : z * rows + kept, :]
        for j in range(rows - kept):
            for i in range(lanes // 128):
                at = j * (lanes // 128) + i
                lay_ref[z, at : at + 1, lanes:] = sum_ref[
                    z * rows + kept + j : z * rows + kept + j + 1, i * 128 : (i + 1) * 128
                ]
    out_ref[:, :, 0:packed] = lay_ref[...].astype(BF16)
    out_ref[:, :, packed:] = caps[...]


def caption_y_kernel(own, *refs):
    ins, out_ref = refs[:Y], refs[Y]
    width = out_ref.shape[2]
    total = None
    for part in ins:
        term = lax.dot_general(
            part[:, width:], part[:, 0:width], (((0,), (0,)), ((), ())), preferred_element_type=F32
        )
        total = term if total is None else total + term
    high = total.astype(BF16).astype(F32)
    low = total - high
    for z in range(Z):
        rows = slice(z * own, (z + 1) * own)
        out_ref[z] = jnp.concatenate([high[rows], low[rows]], axis=0).astype(BF16)


def along_z_kernel(lanes, packed, in_ref, captions, grad_ref, loss_ref, cap_ref, sum_ref, turn_ref):
    rows, cols = grad_ref.shape[1:]
    kept = in_ref.shape[1]
    own, width = captions.shape
    total = in_ref[0].astype(F32)
    for z in range(1, Z):
        total = total + in_ref[z].astype(F32)
    sum_ref[0:kept, :] = total
    for j in range(rows - kept):
        for i in range(lanes // 128):
            at = j * (lanes // 128) + i
            sum_ref[kept + j : kept + j + 1, i * 128 : (i + 1) * 128] = sum_ref[at : at + 1, lanes:packed]
    for k in range(3):
        grad_ref[k] = sum_ref[0:rows, k * cols : (k + 1) * cols]
    loss_ref[...] = jnp.sum(sum_ref[0:1, 3 * cols : 3 * cols + 3], axis=1, keepdims=True)
    frame = whereabouts()[0]
    for f in range(len(ORDER)):

        @pl.when(frame == f)
        def _():
            for i, j in enumerate(ORDER):
                g = f ^ j
                at = packed + i * cols
                turn_ref[:, g * cols : (g + 1) * cols] = (
                    sum_ref[0:own, at : at + cols] + sum_ref[own : 2 * own, at : at + cols]
                )

    dv = turn_ref[...]
    cnorm, unit = norm_of(captions[...])
    cap_ref[...] = (dv - unit * jnp.sum(unit * dv, axis=1, keepdims=True)) / cnorm


ORDER = (0, CORE, 1, CORE ^ 1)


def norm_of(captions):
    capf = captions.astype(F32)
    cnorm = jnp.sqrt(jnp.sum(capf * capf, axis=1, keepdims=True) + 1e-06)
    return cnorm, capf / cnorm


def column(values):
    count = values.shape[1]
    row = lax.broadcasted_iota(jnp.int32, (count, count), 0)
    lane = lax.broadcasted_iota(jnp.int32, (count, count), 1)
    spread = jnp.where(row == lane, values.astype(F32), 0.0)
    return jnp.sum(spread, axis=1, keepdims=True).astype(jnp.int32)


def caption_kernel(captions, out_ref, unit_ref, turn_ref):
    frame = whereabouts()[0]
    cols = captions.shape[1] // len(ORDER)
    unit_ref[...] = norm_of(captions[...])[1]
    for f in range(len(ORDER)):

        @pl.when(frame == f)
        def _():
            for i, j in enumerate(ORDER):
                g = f ^ j
                turn_ref[:, i * cols : (i + 1) * cols] = unit_ref[:, g * cols : (g + 1) * cols]

    low = turn_ref[...].astype(BF16)
    out_ref[...] = jnp.broadcast_to(low[None], out_ref.shape)


def stage_kernel(wide, positive, across, weights, *refs):
    ins, (out_ref, far_ref, w_ref, near_ref, pos_ref, sem, w_sem) = refs[:-7], refs[-7:]
    frame, half, _, _ = whereabouts()
    copies = []
    for k in range(3):
        for i in range(XL):
            start = pl.multiple_of((frame ^ (i * CORE)) * (wide - 128), 128)
            copies.append(
                pltpu.make_async_copy(
                    weights.at[k, :, pl.ds(start, wide)], w_ref.at[k, :, pl.ds(i * wide, wide)], w_sem.at[k, i]
                )
            )
    load = pltpu.make_async_copy(positive, pos_ref, sem.at[len(ins) + 1])
    copies = [pltpu.make_async_copy(piece, out_ref.at[i], sem.at[i]) for i, piece in enumerate(ins)] + copies
    load.start()
    for copy in copies:
        copy.start()
    load.wait()
    first = jnp.where(half == 0, pos_ref[...], across[...])
    second = jnp.where(half == 0, across[...], pos_ref[...])
    near_ref[...] = jnp.concatenate([column(first), column(second)], axis=0)
    copies.append(pltpu.make_async_copy(near_ref, far_ref, sem.at[len(ins)]))
    copies[-1].start()
    for copy in copies:
        copy.wait()


def on_device(frames, conv_weight, captions, positive):
    clip_dev, fr_dev, width = frames.shape
    cap_dev = captions.shape[0]
    cols = width // (XL * CORE)
    group = clip_dev * XH
    rows = FRAMES * group

    positive = positive[None, :]
    across = swap(positive, 1, 0, 0)
    mine = jnp.transpose(frames, (1, 0, 2))
    (spread,) = call(
        caption_kernel,
        4,
        [((Y * Z, cap_dev, width), BF16)],
        [pltpu.VMEM((cap_dev, width), F32), pltpu.VMEM((cap_dev, width), F32)],
        0,
        Y * Z * cap_dev * width * 2,
        captions,
    )
    mine, across, spread = lax.optimization_barrier((mine, across, spread))
    first = swap(mine, 0, 0, 1)
    far = [swap(mine, 0, 1, 0), swap(mine, 1, 0, 0), swap(mine, 1, 1, 0)]
    near = [first] + [swap(part, 0, 0, 1) for part in far]
    wide = cols + (XL * CORE - 1) * (cols % 128)
    held, wanted, weights = call(
        functools.partial(stage_kernel, wide),
        2,
        [((3,) + mine.shape, BF16), ((group, 1), jnp.int32), ((3, width, XL * wide), BF16)],
        [
            pltpu.VMEM((group, 1), jnp.int32),
            pltpu.VMEM(positive.shape, jnp.int32),
            pltpu.SemaphoreType.DMA((5,)),
            pltpu.SemaphoreType.DMA((3, XL)),
        ],
        0,
        mine.size * 12,
        positive,
        across,
        conv_weight,
        *far,
        loose={0: pltpu.HBM, 2: pltpu.HBM} | {i: pl.ANY for i in range(3, 6)},
        far={0: pltpu.HBM, 1: pltpu.HBM},
    )
    pieces = [mine, *near, held]

    piece = exchange(spread, YZ_GROUPS).reshape(Y * Z * cap_dev, width)
    count = piece.shape[0]
    x, slope, pooled = call(
        functools.partial(conv_kernel, cols),
        24,
        [((FRAMES + 2, group, width), BF16), ((FRAMES, group, wide), F32), ((group, XL * cols), F32)],
        [
            pltpu.VMEM((FRAMES, group, wide), F32),
            pltpu.VMEM((group, width), F32),
            pltpu.VMEM((group, XL * wide), F32),
            pltpu.VMEM((group, XL * cols), F32),
            pltpu.SemaphoreType.DMA((8,)),
            pltpu.SemaphoreType.DMA((FRAMES // fr_dev + 1,)),
        ],
        int(3.5 * rows * 3 * width * 2 * cols),
        3 * width * 2 * wide * 2,
        *pieces,
        weights,
        loose={i: pl.ANY for i in range(5)} | {5: pltpu.HBM},
        far={1: pltpu.HBM, 2: pltpu.HBM},
    )
    pooled, piece = lax.optimization_barrier((pooled, piece))
    peer = swap(pooled, 0, 0, 1)
    lanes = roundup(2 * cols + 2, 128)
    keep, send, unit, pnorm, *dv = call(
        functools.partial(pair_kernel, cap_dev),
        8,
        [((group, lanes), F32), ((group, lanes), F32), ((group, cols), F32), ((group, 1), F32)]
        + [((group, width + roundup(count // Y, 128)), BF16)] * Y,
        [
            pltpu.VMEM((group, width), F32),
            pltpu.VMEM((Y, group, roundup(count // Y, 128)), BF16),
            pltpu.VMEM((group, 2 * cols), F32),
            pltpu.VMEM((group, 1), jnp.int32),
            pltpu.SemaphoreType.DMA((2,)),
        ],
        6 * group * count * width,
        count * width * 6,
        pooled,
        peer,
        piece,
        wanted,
        loose={0: pltpu.HBM, 3: pltpu.HBM},
    )

    chip = keep + swap(send, 0, 0, 1)
    tail = chip[:, 2 * cols : 2 * cols + 2]
    spare = jnp.zeros((group, roundup(cols + 2, 128) - cols - 2), F32)
    same = jnp.concatenate([chip[:, :cols], tail, spare], axis=1)
    cross = jnp.concatenate([chip[:, cols : 2 * cols], tail, spare], axis=1)
    same, cross, x = lax.optimization_barrier((same, cross, x))
    parts = [same, swap(same, 1, 0, 0), swap(cross, 0, 1, 0), swap(cross, 1, 1, 0)]

    share = width // XH // Y
    (x,) = call(
        turn_kernel,
        6,
        [((roundup(Y * share, 128), rows + 2 * group), BF16)],
        [],
        0,
        rows * width * 2,
        x,
    )
    x, *dv = lax.optimization_barrier((x, *dv))
    packed = roundup(3 * cols + 3, 128)
    terms = call(
        weight_kernel,
        16,
        [((share, packed), BF16)] * Y,
        [
            pltpu.VMEM((rows + 2 * group, 3 * wide), BF16),
            pltpu.VMEM((roundup(Y * share, 128), 3 * wide), F32),
            pltpu.VMEM((group, wide), F32),
            pltpu.VMEM((share, packed), F32),
            pltpu.VMEM((FRAMES, group, wide), F32),
            pltpu.SemaphoreType.DMA(()),
        ],
        6 * rows * Y * share * cols,
        rows * width * 2,
        *parts,
        unit,
        pnorm,
        slope,
        x,
        loose={6: pltpu.HBM},
    )
    dv = [dv[0]] + [move(dv[i], i, 0) for i in range(1, Y)]
    *dv, first = lax.optimization_barrier((*dv, terms[1]))
    terms = [terms[0], first, *terms[2:]]
    (dv,) = call(
        functools.partial(caption_y_kernel, cap_dev),
        6,
        [((Z, 2 * cap_dev, width), BF16)],
        [],
        2 * count * group * width,
        count * width * 4,
        *dv,
    )
    terms = [terms[0]] + [move(terms[i], i, 0) for i in range(1, Y)]
    own_rows = share // Z
    kept = own_rows // 16 * 16
    (terms,) = call(
        functools.partial(along_y_kernel, 3 * cols),
        8,
        [((Z, kept, packed + 128 + width), BF16)],
        [pltpu.VMEM((share, packed), F32), pltpu.VMEM((Z, kept, packed + 128), F32)],
        0,
        share * packed * 16,
        *terms,
        dv,
    )
    terms = exchange(terms, Z_GROUPS)
    grad_weight, loss, grad_captions = call(
        functools.partial(along_z_kernel, packed, packed + 128),
        4,
        [((3, own_rows, cols), F32), ((1, 1), F32), ((cap_dev, width), F32)],
        [pltpu.VMEM((roundup(own_rows, 8), packed + 128 + width), F32), pltpu.VMEM((cap_dev, width), F32)],
        0,
        share * packed * 2,
        terms,
        captions,
    )
    loss = loss[0, 0] / (clip_dev * lax.axis_size("clip"))
    return (loss, grad_weight, grad_captions)


def solution(mesh):
    placed = (P("clip", "frame", None), P(), P(("clip", "frame"), None), P("clip"))
    return jax.shard_map(
        on_device,
        mesh=mesh,
        in_specs=placed,
        out_specs=(P(), P(None, "clip", "frame"), P(("clip", "frame"), None)),
        check_vma=False,
    )
```

```python
import functools
import math

import jax
import jax.numpy as jnp
from jax import lax
from jax.experimental import pallas as pl
from jax.experimental.pallas import tpu as pltpu
from jax.sharding import PartitionSpec as P

FRAMES = 16
XH, Y, Z, XL, CORE = 2, 4, 8, 2, 2
BOTH = ("clip", "frame")
F32, BF16 = jnp.float32, jnp.bfloat16
ROOT = math.sqrt(2.0 / math.pi)
CUBE = 0.044715


def place(index):
    clip, frame = divmod(index, XL * CORE)
    xh, rest = divmod(clip, Y * Z)
    y, z = divmod(rest, Z)
    xl, core = divmod(frame, CORE)
    return xh, y, z, xl, core


def index_of(xh, y, z, xl, core):
    return (((xh * Y + y) * Z + z) * XL + xl) * CORE + core


def swap(value, flip_xh, flip_xl, flip_core):
    pairs = []
    for source in range(XH * Y * Z * XL * CORE):
        xh, y, z, xl, core = place(source)
        pairs.append((source, index_of(xh ^ flip_xh, y, z, xl ^ flip_xl, core ^ flip_core)))
    return lax.ppermute(value, BOTH, pairs)


def move(value, by_y, by_z):
    pairs = []
    for source in range(XH * Y * Z * XL * CORE):
        xh, y, z, xl, core = place(source)
        pairs.append((source, index_of(xh, (y + by_y) % Y, (z + by_z) % Z, xl, core)))
    return lax.ppermute(value, BOTH, pairs)


Z_GROUPS = [[(xh * Y + y) * Z + z for z in range(Z)] for xh in range(XH) for y in range(Y)]
YZ_GROUPS = [[xh * Y * Z + yz for yz in range(Y * Z)] for xh in range(XH)]


def exchange(value, groups):
    return lax.all_to_all(value, "clip", 0, 0, axis_index_groups=groups, tiled=True)


def roundup(value, unit):
    return -(-value // unit) * unit


def whereabouts():
    clip = lax.axis_index("clip")
    return lax.axis_index("frame"), clip // (Y * Z), clip // Z % Y, clip % Z


def call(body, mib, out_shapes, scratch, flops, moved, *operands, loose={}, far={}):
    specs = []
    operands = list(operands)
    for i, o in enumerate(operands):
        space = loose.get(i, pltpu.VMEM)
        if space is pltpu.HBM:
            operands[i] = pltpu.with_memory_space_constraint(o, space)
        specs.append(pl.BlockSpec(memory_space=space))
    return pl.pallas_call(
        body,
        out_shape=[
            far[i](s, d) if i in far else jax.ShapeDtypeStruct(s, d) for i, (s, d) in enumerate(out_shapes)
        ],
        in_specs=specs,
        out_specs=[pl.BlockSpec(memory_space=far.get(i, pltpu.VMEM)) for i in range(len(out_shapes))],
        scratch_shapes=scratch,
        cost_estimate=pl.CostEstimate(flops=flops, bytes_accessed=moved, transcendentals=0),
        compiler_params=pltpu.CompilerParams(vmem_limit_bytes=mib * 2**20),
    )(*operands)


def conv_kernel(cols, *refs):
    (mine, *near, held), (w_ref, positive, across), rest = (
        refs[:6],
        refs[6:9],
        refs[9:],
    )
    x_ref, out_ref, mean_ref, wanted_ref, slope_ref, sum_ref, part_ref, pooled_ref, id_ref, pos_ref, x_sem, o_sem = rest
    far = [mine] + [held.at[i] for i in range(held.shape[0])]
    pieces = [far[0], near[0], far[1], near[1], far[2], near[2], far[3], near[3]]
    frame, half, _, _ = whereabouts()
    steps, block, width = mine.shape
    group = pooled_ref.shape[0]
    wide = slope_ref.shape[2]
    copies = []
    for i, piece in enumerate(pieces):
        j, side = i % 4, i // 4
        first = (frame ^ j) * steps + 1
        start = pl.multiple_of((half ^ side) * block, block)
        copies.append(
            pltpu.make_async_copy(
                piece, x_ref.at[pl.ds(first, steps), pl.ds(start, block), :], x_sem.at[i]
            )
        )
    load = pltpu.make_async_copy(positive, pos_ref, o_sem.at[FRAMES // steps + 1])
    load.start()
    for copy in copies:
        copy.start()
    x_ref[0] = jnp.zeros((group, width), BF16)
    x_ref[FRAMES + 1] = jnp.zeros((group, width), BF16)
    sum_ref[...] = jnp.zeros_like(sum_ref)
    part_ref[...] = jnp.zeros_like(part_ref)
    load.wait()
    first = jnp.where(half == 0, pos_ref[...], across[...])
    second = jnp.where(half == 0, across[...], pos_ref[...])
    id_ref[...] = jnp.concatenate([column(first), column(second)], axis=0)
    stores = [pltpu.make_async_copy(id_ref, wanted_ref, o_sem.at[FRAMES // steps + 1])]
    stores[0].start()
    for copy in copies:
        copy.wait()

    def step(m):
        base = m * steps
        conv = None
        for k in range(3):
            rows = x_ref[pl.ds(base + k, steps)].reshape(steps * group, width)
            term = jnp.dot(rows, w_ref[k], preferred_element_type=F32)
            conv = term if conv is None else conv + term
        tanh = jnp.tanh(conv * (ROOT + (ROOT * CUBE) * (conv * conv)))
        part = 0.5 * conv
        gelu = part + part * tanh
        part_ref[...] += jnp.sum(gelu.reshape(steps, group, XL * wide), axis=0)
        conv, tanh, part = conv[:, :wide], tanh[:, :wide], part[:, :wide]
        slope = 0.5 * (1.0 + tanh) + part * (1.0 - tanh * tanh) * (
            ROOT + (3.0 * ROOT * CUBE) * (conv * conv)
        )
        slope_ref[pl.ds(base, steps)] = slope.reshape(steps, group, wide)
        sum_ref[...] += jnp.sum(x_ref[pl.ds(base + 1, steps)].astype(F32), axis=0)

    for m in range(FRAMES // steps):
        step(m)
        rows = pl.ds(m * steps, steps)
        stores.append(pltpu.make_async_copy(slope_ref.at[rows], out_ref.at[rows], o_sem.at[m]))
        stores[-1].start()
    shift = cols + 128 - wide
    for f in range(XL * CORE):

        @pl.when(frame == f)
        def _():
            for i in range(XL):
                g = f ^ (i * CORE)
                gelu = part_ref[:, i * wide + g * shift : i * wide + g * shift + cols]
                pooled_ref[:, i * cols : (i + 1) * cols] = (
                    sum_ref[:, g * cols : (g + 1) * cols] + gelu
                ) / FRAMES

    stores.append(pltpu.make_async_copy(pooled_ref, mean_ref, o_sem.at[FRAMES // steps]))
    stores[-1].start()
    for store in stores:
        store.wait()


def pair_kernel(cap_dev, pooled_in, peer, v_ref, wanted, *refs):
    (keep_ref, send_ref, unit_ref, norm_ref), dv_refs, (pooled_ref, lay_ref, mine, near_ref, sem) = refs[:4], refs[4 : 4 + Y], refs[4 + Y :]
    first = pltpu.make_async_copy(pooled_in, mine, sem.at[0])
    first.start()
    load = pltpu.make_async_copy(wanted, near_ref, sem.at[1])
    load.start()
    first.wait()
    frame, half, y_pos, _ = whereabouts()
    part = mine.shape[1]
    cols = part // 2
    group = mine.shape[0]
    pooled_ref[:, 0:part] = mine[...]
    pooled_ref[:, part : 2 * part] = peer[...]
    pooled = pooled_ref[...]
    pnorm = jnp.sqrt(jnp.sum(pooled * pooled, axis=1, keepdims=True) + 1e-06)
    unit = pooled / pnorm
    u_low = unit.astype(BF16)
    v_low = v_ref[...]
    dots = lax.dot_general(u_low, v_low, (((1,), (1,)), ((), ())), preferred_element_type=F32)
    logits = 10.0 * dots - 10.0
    row = lax.broadcasted_iota(jnp.int32, (1, v_low.shape[0]), 1)
    ids = ((half * (Y * Z) + row // cap_dev) * (XL * CORE) + frame) * cap_dev + row % cap_dev
    load.wait()
    match = jnp.where(near_ref[...] == ids, 1.0, 0.0).astype(F32)
    sign = 2.0 * match - 1.0
    turned = -sign * logits
    terms = jnp.maximum(turned, 0.0) + jnp.log1p(jnp.exp(-jnp.abs(turned)))
    total = jnp.sum(jnp.sum(terms, axis=1, keepdims=True), axis=0, keepdims=True)
    grad = 10.0 * (1.0 / (1.0 + jnp.exp(-logits)) - match)
    coef = grad.astype(BF16)
    du = jnp.dot(coef, v_low, preferred_element_type=F32)
    share = coef.shape[1] // Y
    for y in range(Y):
        block = grad[:, y * share : (y + 1) * share]
        pad = jnp.zeros((group, lay_ref.shape[2] - share), F32)
        lay_ref[y] = jnp.concatenate([block, pad], axis=1).astype(BF16)
    for i, dv_ref in enumerate(dv_refs):
        dv_ref[:, 0 : 2 * part] = u_low
        dv_ref[:, 2 * part :] = lay_ref[(y_pos + i) % Y]
    along = jnp.sum(unit * du, axis=1, keepdims=True)
    pooled_ref[...] = du
    spare = keep_ref.shape[1] - part
    lane = lax.broadcasted_iota(jnp.int32, (group, spare), 1)
    tail = jnp.where(lane == 0, along, jnp.where(lane == 1, total, 0.0))
    keep_ref[:, 0:part] = pooled_ref[:, 0:part]
    send_ref[:, 0:part] = pooled_ref[:, part : 2 * part]
    keep_ref[:, part:] = tail
    send_ref[:, part:] = tail
    unit_ref[...] = unit[:, 0:cols]
    norm_ref[...] = pnorm


def turn_kernel(x_ref, out_ref):
    half = whereabouts()[1]
    tile = 128
    tiles = out_ref.shape[0] // tile
    offset = x_ref.shape[2] - tiles * tile
    for m in range(tiles):
        start = pl.multiple_of(half * offset + m * tile, tile)
        rows = x_ref[:, :, pl.ds(start, tile)].reshape(x_ref.shape[0] * x_ref.shape[1], tile)
        out_ref[m * tile : (m + 1) * tile, :] = rows.T


def weight_kernel(s0, s1, s2, s3, unit, norm, slope_in, x_ref, *refs):
    outs, (d_ref, g_ref, p_ref, c_ref, slope, sem) = refs[:Y], refs[Y:]
    load = pltpu.make_async_copy(slope_in, slope, sem)
    load.start()
    frame, half, y_pos, _ = whereabouts()
    group, cols = unit.shape
    wide = slope.shape[2]
    shift = cols + 128 - wide
    share = outs[0].shape[0]
    full = s0[...] + s1[...] + s2[...] + s3[...]
    along, total = full[:, cols : cols + 1], full[0:1, cols + 1 : cols + 2]
    dpooled = (full[:, 0:cols] - unit[...] * along) / norm[...] / FRAMES
    p_ref[...] = jnp.zeros_like(p_ref)
    for f in range(XL * CORE):

        @pl.when(frame == f)
        def _():
            p_ref[:, f * shift : f * shift + cols] = dpooled

    dpooled = p_ref[...]
    zero = jnp.zeros((group, wide), BF16)
    for k in range(3):
        for t in range(FRAMES + 2):
            if t < k or t >= FRAMES + k:
                d_ref[t * group : (t + 1) * group, k * wide : (k + 1) * wide] = zero
    load.wait()
    for t in range(FRAMES):
        dconv = (slope[t] * dpooled).astype(BF16)
        for k in range(3):
            d_ref[(t + k) * group : (t + k + 1) * group, k * wide : (k + 1) * wide] = dconv
    g_ref[...] = jnp.dot(x_ref[...], d_ref[...], preferred_element_type=F32)
    skip = x_ref.shape[0] - Y * share
    lane = lax.broadcasted_iota(jnp.int32, (share, c_ref.shape[1] - 3 * cols), 1)
    c_ref[:, 3 * cols :] = loss_lanes(total, lane)
    for i, out_ref in enumerate(outs):
        start = pl.multiple_of(half * skip + ((y_pos + i) % Y) * share, 16)
        for f in range(XL * CORE):

            @pl.when(frame == f)
            def _():
                for k in range(3):
                    c_ref[:, k * cols : (k + 1) * cols] = g_ref[
                        pl.ds(start, share), k * wide + f * shift : k * wide + f * shift + cols
                    ]

        out_ref[...] = c_ref[...].astype(BF16)


def loss_lanes(total, lane):
    first = total.astype(BF16).astype(F32)
    second = (total - first).astype(BF16).astype(F32)
    third = total - first - second
    return jnp.where(lane == 0, first, jnp.where(lane == 1, second, jnp.where(lane == 2, third, 0.0)))


def along_y_kernel(first_lane, *refs):
    ins, caps, (out_ref, sum_ref, lay_ref) = refs[:Y], refs[Y], refs[Y + 1 :]
    rows, lanes = ins[0].shape[0] // Z, ins[0].shape[1]
    kept, packed = lay_ref.shape[1:]
    total = ins[0][...].astype(F32)
    for part in ins[1:]:
        total = total + part[...].astype(F32)
    sum_ref[...] = total
    loss = jnp.sum(sum_ref[0:1, first_lane : first_lane + 3], axis=1, keepdims=True)
    lane = lax.broadcasted_iota(jnp.int32, (1, lanes - first_lane), 1)
    tail = loss_lanes(loss, lane)
    lay_ref[...] = jnp.zeros_like(lay_ref)
    for z in range(Z):
        sum_ref[z * rows : z * rows + 1, first_lane:] = tail
        lay_ref[z, :, 0:lanes] = sum_ref[z * rows : z * rows + kept, :]
        for j in range(rows - kept):
            for i in range(lanes // 128):
                at = j * (lanes // 128) + i
                lay_ref[z, at : at + 1, lanes:] = sum_ref[
                    z * rows + kept + j : z * rows + kept + j + 1, i * 128 : (i + 1) * 128
                ]
    out_ref[:, :, 0:packed] = lay_ref[...].astype(BF16)
    out_ref[:, :, packed:] = caps[...]


def caption_y_kernel(own, *refs):
    ins, out_ref = refs[:Y], refs[Y]
    width = out_ref.shape[2]
    total = None
    for part in ins:
        term = lax.dot_general(
            part[:, width:], part[:, 0:width], (((0,), (0,)), ((), ())), preferred_element_type=F32
        )
        total = term if total is None else total + term
    high = total.astype(BF16).astype(F32)
    low = total - high
    for z in range(Z):
        rows = slice(z * own, (z + 1) * own)
        out_ref[z] = jnp.concatenate([high[rows], low[rows]], axis=0).astype(BF16)


def along_z_kernel(lanes, packed, in_ref, captions, grad_ref, loss_ref, cap_ref, sum_ref, turn_ref):
    rows, cols = grad_ref.shape[1:]
    kept = in_ref.shape[1]
    own, width = captions.shape
    total = in_ref[0].astype(F32)
    for z in range(1, Z):
        total = total + in_ref[z].astype(F32)
    sum_ref[0:kept, :] = total
    for j in range(rows - kept):
        for i in range(lanes // 128):
            at = j * (lanes // 128) + i
            sum_ref[kept + j : kept + j + 1, i * 128 : (i + 1) * 128] = sum_ref[at : at + 1, lanes:packed]
    for k in range(3):
        grad_ref[k] = sum_ref[0:rows, k * cols : (k + 1) * cols]
    loss_ref[...] = jnp.sum(sum_ref[0:1, 3 * cols : 3 * cols + 3], axis=1, keepdims=True)
    frame = whereabouts()[0]
    for f in range(len(ORDER)):

        @pl.when(frame == f)
        def _():
            for i, j in enumerate(ORDER):
                g = f ^ j
                at = packed + i * cols
                turn_ref[:, g * cols : (g + 1) * cols] = (
                    sum_ref[0:own, at : at + cols] + sum_ref[own : 2 * own, at : at + cols]
                )

    dv = turn_ref[...]
    cnorm, unit = norm_of(captions[...])
    cap_ref[...] = (dv - unit * jnp.sum(unit * dv, axis=1, keepdims=True)) / cnorm


ORDER = (0, CORE, 1, CORE ^ 1)


def norm_of(captions):
    capf = captions.astype(F32)
    cnorm = jnp.sqrt(jnp.sum(capf * capf, axis=1, keepdims=True) + 1e-06)
    return cnorm, capf / cnorm


def column(values):
    count = values.shape[1]
    row = lax.broadcasted_iota(jnp.int32, (count, count), 0)
    lane = lax.broadcasted_iota(jnp.int32, (count, count), 1)
    spread = jnp.where(row == lane, values.astype(F32), 0.0)
    return jnp.sum(spread, axis=1, keepdims=True).astype(jnp.int32)


def caption_kernel(captions, out_ref, unit_ref, turn_ref):
    frame = whereabouts()[0]
    cols = captions.shape[1] // len(ORDER)
    unit_ref[...] = norm_of(captions[...])[1]
    for f in range(len(ORDER)):

        @pl.when(frame == f)
        def _():
            for i, j in enumerate(ORDER):
                g = f ^ j
                turn_ref[:, i * cols : (i + 1) * cols] = unit_ref[:, g * cols : (g + 1) * cols]

    low = turn_ref[...].astype(BF16)
    out_ref[...] = jnp.broadcast_to(low[None], out_ref.shape)


def stage_kernel(wide, weights, *refs):
    ins, (out_ref, w_ref, sem, w_sem) = refs[:-4], refs[-4:]
    frame = whereabouts()[0]
    copies = [pltpu.make_async_copy(piece, out_ref.at[i], sem.at[i]) for i, piece in enumerate(ins)]
    for k in range(3):
        for i in range(XL):
            start = pl.multiple_of((frame ^ (i * CORE)) * (wide - 128), 128)
            copies.append(
                pltpu.make_async_copy(
                    weights.at[k, :, pl.ds(start, wide)], w_ref.at[k, :, pl.ds(i * wide, wide)], w_sem.at[k, i]
                )
            )
    for copy in copies:
        copy.start()
    for copy in copies:
        copy.wait()


def on_device(frames, conv_weight, captions, positive):
    clip_dev, fr_dev, width = frames.shape
    cap_dev = captions.shape[0]
    cols = width // (XL * CORE)
    group = clip_dev * XH
    rows = FRAMES * group

    positive = positive[None, :]
    across = swap(positive, 1, 0, 0)
    mine = jnp.transpose(frames, (1, 0, 2))
    (spread,) = call(
        caption_kernel,
        4,
        [((Y * Z, cap_dev, width), BF16)],
        [pltpu.VMEM((cap_dev, width), F32), pltpu.VMEM((cap_dev, width), F32)],
        0,
        Y * Z * cap_dev * width * 2,
        captions,
    )
    first = swap(mine, 0, 0, 1)
    far = [swap(mine, 0, 1, 0), swap(mine, 1, 0, 0), swap(mine, 1, 1, 0)]
    near = [first] + [swap(part, 0, 0, 1) for part in far]
    wide = cols + (XL * CORE - 1) * (cols % 128)
    held, weights = call(
        functools.partial(stage_kernel, wide),
        2,
        [((3,) + mine.shape, BF16), ((3, width, XL * wide), BF16)],
        [pltpu.SemaphoreType.DMA((3,)), pltpu.SemaphoreType.DMA((3, XL))],
        0,
        mine.size * 12,
        conv_weight,
        *far,
        loose={0: pltpu.HBM} | {i: pl.ANY for i in range(1, 4)},
        far={0: pltpu.HBM},
    )
    pieces = [mine, *near, held]

    piece = exchange(spread, YZ_GROUPS).reshape(Y * Z * cap_dev, width)
    count = piece.shape[0]
    x, slope, pooled, wanted = call(
        functools.partial(conv_kernel, cols),
        24,
        [((FRAMES + 2, group, width), BF16), ((FRAMES, group, wide), F32), ((group, XL * cols), F32)]
        + [((group, 1), jnp.int32)],
        [
            pltpu.VMEM((FRAMES, group, wide), F32),
            pltpu.VMEM((group, width), F32),
            pltpu.VMEM((group, XL * wide), F32),
            pltpu.VMEM((group, XL * cols), F32),
            pltpu.VMEM((group, 1), jnp.int32),
            pltpu.VMEM(positive.shape, jnp.int32),
            pltpu.SemaphoreType.DMA((8,)),
            pltpu.SemaphoreType.DMA((FRAMES // fr_dev + 2,)),
        ],
        int(3.5 * rows * 3 * width * 2 * cols),
        3 * width * 2 * wide * 2,
        *pieces,
        weights,
        positive,
        across,
        loose={i: pl.ANY for i in range(5)} | {5: pltpu.HBM, 7: pltpu.HBM},
        far={1: pltpu.HBM, 2: pltpu.HBM, 3: pltpu.HBM},
    )
    pooled, piece = lax.optimization_barrier((pooled, piece))
    peer = swap(pooled, 0, 0, 1)
    lanes = roundup(2 * cols + 2, 128)
    keep, send, unit, pnorm, *dv = call(
        functools.partial(pair_kernel, cap_dev),
        8,
        [((group, lanes), F32), ((group, lanes), F32), ((group, cols), F32), ((group, 1), F32)]
        + [((group, width + roundup(count // Y, 128)), BF16)] * Y,
        [
            pltpu.VMEM((group, width), F32),
            pltpu.VMEM((Y, group, roundup(count // Y, 128)), BF16),
            pltpu.VMEM((group, 2 * cols), F32),
            pltpu.VMEM((group, 1), jnp.int32),
            pltpu.SemaphoreType.DMA((2,)),
        ],
        6 * group * count * width,
        count * width * 6,
        pooled,
        peer,
        piece,
        wanted,
        loose={0: pltpu.HBM, 3: pltpu.HBM},
    )

    chip = keep + swap(send, 0, 0, 1)
    tail = chip[:, 2 * cols : 2 * cols + 2]
    spare = jnp.zeros((group, roundup(cols + 2, 128) - cols - 2), F32)
    same = jnp.concatenate([chip[:, :cols], tail, spare], axis=1)
    cross = jnp.concatenate([chip[:, cols : 2 * cols], tail, spare], axis=1)
    same, cross, x = lax.optimization_barrier((same, cross, x))
    parts = [same, swap(same, 1, 0, 0), swap(cross, 0, 1, 0), swap(cross, 1, 1, 0)]

    share = width // XH // Y
    (x,) = call(
        turn_kernel,
        6,
        [((roundup(Y * share, 128), rows + 2 * group), BF16)],
        [],
        0,
        rows * width * 2,
        x,
    )
    x, *dv = lax.optimization_barrier((x, *dv))
    packed = roundup(3 * cols + 3, 128)
    terms = call(
        weight_kernel,
        16,
        [((share, packed), BF16)] * Y,
        [
            pltpu.VMEM((rows + 2 * group, 3 * wide), BF16),
            pltpu.VMEM((roundup(Y * share, 128), 3 * wide), F32),
            pltpu.VMEM((group, wide), F32),
            pltpu.VMEM((share, packed), F32),
            pltpu.VMEM((FRAMES, group, wide), F32),
            pltpu.SemaphoreType.DMA(()),
        ],
        6 * rows * Y * share * cols,
        rows * width * 2,
        *parts,
        unit,
        pnorm,
        slope,
        x,
        loose={6: pltpu.HBM},
    )
    dv = [dv[0]] + [move(dv[i], i, 0) for i in range(1, Y)]
    *dv, first = lax.optimization_barrier((*dv, terms[1]))
    terms = [terms[0], first, *terms[2:]]
    (dv,) = call(
        functools.partial(caption_y_kernel, cap_dev),
        6,
        [((Z, 2 * cap_dev, width), BF16)],
        [],
        2 * count * group * width,
        count * width * 4,
        *dv,
    )
    terms = [terms[0]] + [move(terms[i], i, 0) for i in range(1, Y)]
    own_rows = share // Z
    kept = own_rows // 16 * 16
    (terms,) = call(
        functools.partial(along_y_kernel, 3 * cols),
        8,
        [((Z, kept, packed + 128 + width), BF16)],
        [pltpu.VMEM((share, packed), F32), pltpu.VMEM((Z, kept, packed + 128), F32)],
        0,
        share * packed * 16,
        *terms,
        dv,
    )
    terms = exchange(terms, Z_GROUPS)
    grad_weight, loss, grad_captions = call(
        functools.partial(along_z_kernel, packed, packed + 128),
        4,
        [((3, own_rows, cols), F32), ((1, 1), F32), ((cap_dev, width), F32)],
        [pltpu.VMEM((roundup(own_rows, 8), packed + 128 + width), F32), pltpu.VMEM((cap_dev, width), F32)],
        0,
        share * packed * 2,
        terms,
        captions,
    )
    loss = loss[0, 0] / (clip_dev * lax.axis_size("clip"))
    return (loss, grad_weight, grad_captions)


def solution(mesh):
    placed = (P("clip", "frame", None), P(), P(("clip", "frame"), None), P("clip"))
    return jax.shard_map(
        on_device,
        mesh=mesh,
        in_specs=placed,
        out_specs=(P(), P(None, "clip", "frame"), P(("clip", "frame"), None)),
        check_vma=False,
    )
```

```python
import functools
import math

import jax
import jax.numpy as jnp
from jax import lax
from jax.experimental import pallas as pl
from jax.experimental.pallas import tpu as pltpu
from jax.sharding import PartitionSpec as P

FRAMES = 16
XH, Y, Z, XL, CORE = 2, 4, 8, 2, 2
BOTH = ("clip", "frame")
F32, BF16 = jnp.float32, jnp.bfloat16
ROOT = math.sqrt(2.0 / math.pi)
CUBE = 0.044715


def place(index):
    clip, frame = divmod(index, XL * CORE)
    xh, rest = divmod(clip, Y * Z)
    y, z = divmod(rest, Z)
    xl, core = divmod(frame, CORE)
    return xh, y, z, xl, core


def index_of(xh, y, z, xl, core):
    return (((xh * Y + y) * Z + z) * XL + xl) * CORE + core


def swap(value, flip_xh, flip_xl, flip_core):
    pairs = []
    for source in range(XH * Y * Z * XL * CORE):
        xh, y, z, xl, core = place(source)
        pairs.append((source, index_of(xh ^ flip_xh, y, z, xl ^ flip_xl, core ^ flip_core)))
    return lax.ppermute(value, BOTH, pairs)


def move(value, by_y, by_z):
    pairs = []
    for source in range(XH * Y * Z * XL * CORE):
        xh, y, z, xl, core = place(source)
        pairs.append((source, index_of(xh, (y + by_y) % Y, (z + by_z) % Z, xl, core)))
    return lax.ppermute(value, BOTH, pairs)


Z_GROUPS = [[(xh * Y + y) * Z + z for z in range(Z)] for xh in range(XH) for y in range(Y)]
YZ_GROUPS = [[xh * Y * Z + yz for yz in range(Y * Z)] for xh in range(XH)]


def exchange(value, groups):
    return lax.all_to_all(value, "clip", 0, 0, axis_index_groups=groups, tiled=True)


def roundup(value, unit):
    return -(-value // unit) * unit


def whereabouts():
    clip = lax.axis_index("clip")
    return lax.axis_index("frame"), clip // (Y * Z), clip // Z % Y, clip % Z


def call(body, mib, out_shapes, scratch, flops, moved, *operands, loose={}, far={}, same={}):
    specs = []
    operands = list(operands)
    for i, o in enumerate(operands):
        space = loose.get(i, pltpu.VMEM)
        if space is pltpu.HBM:
            operands[i] = pltpu.with_memory_space_constraint(o, space)
        specs.append(pl.BlockSpec(memory_space=space))
    return pl.pallas_call(
        body,
        out_shape=[
            far[i](s, d) if i in far else jax.ShapeDtypeStruct(s, d) for i, (s, d) in enumerate(out_shapes)
        ],
        in_specs=specs,
        out_specs=[pl.BlockSpec(memory_space=far.get(i, pltpu.VMEM)) for i in range(len(out_shapes))],
        scratch_shapes=scratch,
        input_output_aliases=same,
        cost_estimate=pl.CostEstimate(flops=flops, bytes_accessed=moved, transcendentals=0),
        compiler_params=pltpu.CompilerParams(vmem_limit_bytes=mib * 2**20),
    )(*operands)


def conv_kernel(cols, *refs):
    near, (_, w_ref, positive, across), rest = refs[:4], refs[4:8], refs[8:]
    x_ref, out_ref, mean_ref, wanted_ref, slope_ref, sum_ref, part_ref, pooled_ref, id_ref, pos_ref, x_sem, o_sem = rest
    frame, half, _, _ = whereabouts()
    steps, block, width = near[0].shape
    group = pooled_ref.shape[0]
    wide = slope_ref.shape[2]
    order = ((1, 0), (CORE ^ 1, 0), (1, 1), (CORE ^ 1, 1))
    copies = placed(dict(zip(order, near)), x_ref, x_sem)
    load = pltpu.make_async_copy(positive, pos_ref, o_sem.at[FRAMES // steps + 1])
    load.start()
    for copy in copies:
        copy.start()
    sum_ref[...] = jnp.zeros_like(sum_ref)
    part_ref[...] = jnp.zeros_like(part_ref)
    load.wait()
    first = jnp.where(half == 0, pos_ref[...], across[...])
    second = jnp.where(half == 0, across[...], pos_ref[...])
    id_ref[...] = jnp.concatenate([column(first), column(second)], axis=0)
    stores = [pltpu.make_async_copy(id_ref, wanted_ref, o_sem.at[FRAMES // steps + 1])]
    stores[0].start()
    for copy in copies:
        copy.wait()

    def step(m):
        base = m * steps
        conv = None
        for k in range(3):
            rows = x_ref[pl.ds(base + k, steps)].reshape(steps * group, width)
            term = jnp.dot(rows, w_ref[k], preferred_element_type=F32)
            conv = term if conv is None else conv + term
        tanh = jnp.tanh(conv * (ROOT + (ROOT * CUBE) * (conv * conv)))
        part = 0.5 * conv
        gelu = part + part * tanh
        part_ref[...] += jnp.sum(gelu.reshape(steps, group, XL * wide), axis=0)
        conv, tanh, part = conv[:, :wide], tanh[:, :wide], part[:, :wide]
        slope = 0.5 * (1.0 + tanh) + part * (1.0 - tanh * tanh) * (
            ROOT + (3.0 * ROOT * CUBE) * (conv * conv)
        )
        slope_ref[pl.ds(base, steps)] = slope.reshape(steps, group, wide)
        sum_ref[...] += jnp.sum(x_ref[pl.ds(base + 1, steps)].astype(F32), axis=0)

    for m in range(FRAMES // steps):
        step(m)
        rows = pl.ds(m * steps, steps)
        stores.append(pltpu.make_async_copy(slope_ref.at[rows], out_ref.at[rows], o_sem.at[m]))
        stores[-1].start()
    shift = cols + 128 - wide
    for f in range(XL * CORE):

        @pl.when(frame == f)
        def _():
            for i in range(XL):
                g = f ^ (i * CORE)
                gelu = part_ref[:, i * wide + g * shift : i * wide + g * shift + cols]
                pooled_ref[:, i * cols : (i + 1) * cols] = (
                    sum_ref[:, g * cols : (g + 1) * cols] + gelu
                ) / FRAMES

    stores.append(pltpu.make_async_copy(pooled_ref, mean_ref, o_sem.at[FRAMES // steps]))
    stores[-1].start()
    for store in stores:
        store.wait()


def pair_kernel(cap_dev, pooled_in, peer, v_ref, wanted, *refs):
    (keep_ref, send_ref, unit_ref, norm_ref), dv_refs, (pooled_ref, lay_ref, mine, near_ref, sem) = refs[:4], refs[4 : 4 + Y], refs[4 + Y :]
    first = pltpu.make_async_copy(pooled_in, mine, sem.at[0])
    first.start()
    load = pltpu.make_async_copy(wanted, near_ref, sem.at[1])
    load.start()
    first.wait()
    frame, half, y_pos, _ = whereabouts()
    part = mine.shape[1]
    cols = part // 2
    group = mine.shape[0]
    pooled_ref[:, 0:part] = mine[...]
    pooled_ref[:, part : 2 * part] = peer[...]
    pooled = pooled_ref[...]
    pnorm = jnp.sqrt(jnp.sum(pooled * pooled, axis=1, keepdims=True) + 1e-06)
    unit = pooled / pnorm
    u_low = unit.astype(BF16)
    v_low = v_ref[...]
    dots = lax.dot_general(u_low, v_low, (((1,), (1,)), ((), ())), preferred_element_type=F32)
    logits = 10.0 * dots - 10.0
    row = lax.broadcasted_iota(jnp.int32, (1, v_low.shape[0]), 1)
    ids = ((half * (Y * Z) + row // cap_dev) * (XL * CORE) + frame) * cap_dev + row % cap_dev
    load.wait()
    match = jnp.where(near_ref[...] == ids, 1.0, 0.0).astype(F32)
    sign = 2.0 * match - 1.0
    turned = -sign * logits
    terms = jnp.maximum(turned, 0.0) + jnp.log1p(jnp.exp(-jnp.abs(turned)))
    total = jnp.sum(jnp.sum(terms, axis=1, keepdims=True), axis=0, keepdims=True)
    grad = 10.0 * (1.0 / (1.0 + jnp.exp(-logits)) - match)
    coef = grad.astype(BF16)
    du = jnp.dot(coef, v_low, preferred_element_type=F32)
    share = coef.shape[1] // Y
    for y in range(Y):
        block = grad[:, y * share : (y + 1) * share]
        pad = jnp.zeros((group, lay_ref.shape[2] - share), F32)
        lay_ref[y] = jnp.concatenate([block, pad], axis=1).astype(BF16)
    for i, dv_ref in enumerate(dv_refs):
        dv_ref[:, 0 : 2 * part] = u_low
        dv_ref[:, 2 * part :] = lay_ref[(y_pos + i) % Y]
    along = jnp.sum(unit * du, axis=1, keepdims=True)
    pooled_ref[...] = du
    spare = keep_ref.shape[1] - part
    lane = lax.broadcasted_iota(jnp.int32, (group, spare), 1)
    tail = jnp.where(lane == 0, along, jnp.where(lane == 1, total, 0.0))
    keep_ref[:, 0:part] = pooled_ref[:, 0:part]
    send_ref[:, 0:part] = pooled_ref[:, part : 2 * part]
    keep_ref[:, part:] = tail
    send_ref[:, part:] = tail
    unit_ref[...] = unit[:, 0:cols]
    norm_ref[...] = pnorm


def turn_kernel(x_ref, out_ref):
    half = whereabouts()[1]
    tile = 128
    tiles = out_ref.shape[0] // tile
    offset = x_ref.shape[2] - tiles * tile
    for m in range(tiles):
        start = pl.multiple_of(half * offset + m * tile, tile)
        rows = x_ref[:, :, pl.ds(start, tile)].reshape(x_ref.shape[0] * x_ref.shape[1], tile)
        out_ref[m * tile : (m + 1) * tile, :] = rows.T


def weight_kernel(s0, s1, s2, s3, unit, norm, slope_in, x_ref, *refs):
    outs, (d_ref, g_ref, p_ref, c_ref, slope, sem) = refs[:Y], refs[Y:]
    load = pltpu.make_async_copy(slope_in, slope, sem)
    load.start()
    frame, half, y_pos, _ = whereabouts()
    group, cols = unit.shape
    wide = slope.shape[2]
    shift = cols + 128 - wide
    share = outs[0].shape[0]
    full = s0[...] + s1[...] + s2[...] + s3[...]
    along, total = full[:, cols : cols + 1], full[0:1, cols + 1 : cols + 2]
    dpooled = (full[:, 0:cols] - unit[...] * along) / norm[...] / FRAMES
    p_ref[...] = jnp.zeros_like(p_ref)
    for f in range(XL * CORE):

        @pl.when(frame == f)
        def _():
            p_ref[:, f * shift : f * shift + cols] = dpooled

    dpooled = p_ref[...]
    zero = jnp.zeros((group, wide), BF16)
    for k in range(3):
        for t in range(FRAMES + 2):
            if t < k or t >= FRAMES + k:
                d_ref[t * group : (t + 1) * group, k * wide : (k + 1) * wide] = zero
    load.wait()
    for t in range(FRAMES):
        dconv = (slope[t] * dpooled).astype(BF16)
        for k in range(3):
            d_ref[(t + k) * group : (t + k + 1) * group, k * wide : (k + 1) * wide] = dconv
    g_ref[...] = jnp.dot(x_ref[...], d_ref[...], preferred_element_type=F32)
    skip = x_ref.shape[0] - Y * share
    lane = lax.broadcasted_iota(jnp.int32, (share, c_ref.shape[1] - 3 * cols), 1)
    c_ref[:, 3 * cols :] = loss_lanes(total, lane)
    for i, out_ref in enumerate(outs):
        start = pl.multiple_of(half * skip + ((y_pos + i) % Y) * share, 16)
        for f in range(XL * CORE):

            @pl.when(frame == f)
            def _():
                for k in range(3):
                    c_ref[:, k * cols : (k + 1) * cols] = g_ref[
                        pl.ds(start, share), k * wide + f * shift : k * wide + f * shift + cols
                    ]

        out_ref[...] = c_ref[...].astype(BF16)


def loss_lanes(total, lane):
    first = total.astype(BF16).astype(F32)
    second = (total - first).astype(BF16).astype(F32)
    third = total - first - second
    return jnp.where(lane == 0, first, jnp.where(lane == 1, second, jnp.where(lane == 2, third, 0.0)))


def along_y_kernel(first_lane, *refs):
    ins, caps, (out_ref, sum_ref, lay_ref) = refs[:Y], refs[Y], refs[Y + 1 :]
    rows, lanes = ins[0].shape[0] // Z, ins[0].shape[1]
    kept, packed = lay_ref.shape[1:]
    total = ins[0][...].astype(F32)
    for part in ins[1:]:
        total = total + part[...].astype(F32)
    sum_ref[...] = total
    loss = jnp.sum(sum_ref[0:1, first_lane : first_lane + 3], axis=1, keepdims=True)
    lane = lax.broadcasted_iota(jnp.int32, (1, lanes - first_lane), 1)
    tail = loss_lanes(loss, lane)
    lay_ref[...] = jnp.zeros_like(lay_ref)
    for z in range(Z):
        sum_ref[z * rows : z * rows + 1, first_lane:] = tail
        lay_ref[z, :, 0:lanes] = sum_ref[z * rows : z * rows + kept, :]
        for j in range(rows - kept):
            for i in range(lanes // 128):
                at = j * (lanes // 128) + i
                lay_ref[z, at : at + 1, lanes:] = sum_ref[
                    z * rows + kept + j : z * rows + kept + j + 1, i * 128 : (i + 1) * 128
                ]
    out_ref[:, :, 0:packed] = lay_ref[...].astype(BF16)
    out_ref[:, :, packed:] = caps[...]


def caption_y_kernel(own, *refs):
    ins, out_ref = refs[:Y], refs[Y]
    width = out_ref.shape[2]
    total = None
    for part in ins:
        term = lax.dot_general(
            part[:, width:], part[:, 0:width], (((0,), (0,)), ((), ())), preferred_element_type=F32
        )
        total = term if total is None else total + term
    high = total.astype(BF16).astype(F32)
    low = total - high
    for z in range(Z):
        rows = slice(z * own, (z + 1) * own)
        out_ref[z] = jnp.concatenate([high[rows], low[rows]], axis=0).astype(BF16)


def along_z_kernel(lanes, packed, in_ref, captions, grad_ref, loss_ref, cap_ref, sum_ref, turn_ref):
    rows, cols = grad_ref.shape[1:]
    kept = in_ref.shape[1]
    own, width = captions.shape
    total = in_ref[0].astype(F32)
    for z in range(1, Z):
        total = total + in_ref[z].astype(F32)
    sum_ref[0:kept, :] = total
    for j in range(rows - kept):
        for i in range(lanes // 128):
            at = j * (lanes // 128) + i
            sum_ref[kept + j : kept + j + 1, i * 128 : (i + 1) * 128] = sum_ref[at : at + 1, lanes:packed]
    for k in range(3):
        grad_ref[k] = sum_ref[0:rows, k * cols : (k + 1) * cols]
    loss_ref[...] = jnp.sum(sum_ref[0:1, 3 * cols : 3 * cols + 3], axis=1, keepdims=True)
    frame = whereabouts()[0]
    for f in range(len(ORDER)):

        @pl.when(frame == f)
        def _():
            for i, j in enumerate(ORDER):
                g = f ^ j
                at = packed + i * cols
                turn_ref[:, g * cols : (g + 1) * cols] = (
                    sum_ref[0:own, at : at + cols] + sum_ref[own : 2 * own, at : at + cols]
                )

    dv = turn_ref[...]
    cnorm, unit = norm_of(captions[...])
    cap_ref[...] = (dv - unit * jnp.sum(unit * dv, axis=1, keepdims=True)) / cnorm


ORDER = (0, CORE, 1, CORE ^ 1)


def norm_of(captions):
    capf = captions.astype(F32)
    cnorm = jnp.sqrt(jnp.sum(capf * capf, axis=1, keepdims=True) + 1e-06)
    return cnorm, capf / cnorm


def column(values):
    count = values.shape[1]
    row = lax.broadcasted_iota(jnp.int32, (count, count), 0)
    lane = lax.broadcasted_iota(jnp.int32, (count, count), 1)
    spread = jnp.where(row == lane, values.astype(F32), 0.0)
    return jnp.sum(spread, axis=1, keepdims=True).astype(jnp.int32)


def caption_kernel(captions, out_ref, unit_ref, turn_ref):
    frame = whereabouts()[0]
    cols = captions.shape[1] // len(ORDER)
    unit_ref[...] = norm_of(captions[...])[1]
    for f in range(len(ORDER)):

        @pl.when(frame == f)
        def _():
            for i, j in enumerate(ORDER):
                g = f ^ j
                turn_ref[:, i * cols : (i + 1) * cols] = unit_ref[:, g * cols : (g + 1) * cols]

    low = turn_ref[...].astype(BF16)
    out_ref[...] = jnp.broadcast_to(low[None], out_ref.shape)


def placed(pieces, x_ref, sem):
    frame, half, _, _ = whereabouts()
    copies = []
    for (j, side), piece in pieces.items():
        steps, block, _ = piece.shape
        first = (frame ^ j) * steps + 1
        start = pl.multiple_of((half ^ side) * block, block)
        copies.append(
            pltpu.make_async_copy(
                piece, x_ref.at[pl.ds(first, steps), pl.ds(start, block), :], sem.at[len(copies)]
            )
        )
    return copies


def stage_kernel(wide, weights, *refs):
    (mine, *far), (x_ref, w_ref, sem, w_sem) = refs[:-4], refs[-4:]
    frame = whereabouts()[0]
    group, width = x_ref.shape[1:]
    copies = []
    for k in range(3):
        for i in range(XL):
            start = pl.multiple_of((frame ^ (i * CORE)) * (wide - 128), 128)
            copies.append(
                pltpu.make_async_copy(
                    weights.at[k, :, pl.ds(start, wide)], w_ref.at[k, :, pl.ds(i * wide, wide)], w_sem.at[k, i]
                )
            )
    copies += placed({(0, 0): mine, (CORE, 0): far[0], (0, 1): far[1], (CORE, 1): far[2]}, x_ref, sem)
    for copy in copies:
        copy.start()
    x_ref[0] = jnp.zeros((group, width), BF16)
    x_ref[FRAMES + 1] = jnp.zeros((group, width), BF16)
    for copy in copies:
        copy.wait()


def on_device(frames, conv_weight, captions, positive):
    clip_dev, fr_dev, width = frames.shape
    cap_dev = captions.shape[0]
    cols = width // (XL * CORE)
    group = clip_dev * XH
    rows = FRAMES * group

    positive = positive[None, :]
    across = swap(positive, 1, 0, 0)
    mine = jnp.transpose(frames, (1, 0, 2))
    (spread,) = call(
        caption_kernel,
        4,
        [((Y * Z, cap_dev, width), BF16)],
        [pltpu.VMEM((cap_dev, width), F32), pltpu.VMEM((cap_dev, width), F32)],
        0,
        Y * Z * cap_dev * width * 2,
        captions,
    )
    first = swap(mine, 0, 0, 1)
    far = [swap(mine, 0, 1, 0), swap(mine, 1, 0, 0), swap(mine, 1, 1, 0)]
    near = [first] + [swap(part, 0, 0, 1) for part in far]
    wide = cols + (XL * CORE - 1) * (cols % 128)
    x, weights = call(
        functools.partial(stage_kernel, wide),
        2,
        [((FRAMES + 2, group, width), BF16), ((3, width, XL * wide), BF16)],
        [pltpu.SemaphoreType.DMA((4,)), pltpu.SemaphoreType.DMA((3, XL))],
        0,
        mine.size * 12,
        conv_weight,
        mine,
        *far,
        loose={0: pltpu.HBM} | {i: pl.ANY for i in range(1, 5)},
    )

    piece = exchange(spread, YZ_GROUPS).reshape(Y * Z * cap_dev, width)
    count = piece.shape[0]
    x, slope, pooled, wanted = call(
        functools.partial(conv_kernel, cols),
        24,
        [((FRAMES + 2, group, width), BF16), ((FRAMES, group, wide), F32), ((group, XL * cols), F32)]
        + [((group, 1), jnp.int32)],
        [
            pltpu.VMEM((FRAMES, group, wide), F32),
            pltpu.VMEM((group, width), F32),
            pltpu.VMEM((group, XL * wide), F32),
            pltpu.VMEM((group, XL * cols), F32),
            pltpu.VMEM((group, 1), jnp.int32),
            pltpu.VMEM(positive.shape, jnp.int32),
            pltpu.SemaphoreType.DMA((4,)),
            pltpu.SemaphoreType.DMA((FRAMES // fr_dev + 2,)),
        ],
        int(3.5 * rows * 3 * width * 2 * cols),
        3 * width * 2 * wide * 2,
        *near,
        x,
        weights,
        positive,
        across,
        same={4: 0},
        loose={i: pl.ANY for i in range(4)} | {6: pltpu.HBM},
        far={1: pltpu.HBM, 2: pltpu.HBM, 3: pltpu.HBM},
    )
    pooled, piece = lax.optimization_barrier((pooled, piece))
    peer = swap(pooled, 0, 0, 1)
    lanes = roundup(2 * cols + 2, 128)
    keep, send, unit, pnorm, *dv = call(
        functools.partial(pair_kernel, cap_dev),
        8,
        [((group, lanes), F32), ((group, lanes), F32), ((group, cols), F32), ((group, 1), F32)]
        + [((group, width + roundup(count // Y, 128)), BF16)] * Y,
        [
            pltpu.VMEM((group, width), F32),
            pltpu.VMEM((Y, group, roundup(count // Y, 128)), BF16),
            pltpu.VMEM((group, 2 * cols), F32),
            pltpu.VMEM((group, 1), jnp.int32),
            pltpu.SemaphoreType.DMA((2,)),
        ],
        6 * group * count * width,
        count * width * 6,
        pooled,
        peer,
        piece,
        wanted,
        loose={0: pltpu.HBM, 3: pltpu.HBM},
    )

    chip = keep + swap(send, 0, 0, 1)
    tail = chip[:, 2 * cols : 2 * cols + 2]
    spare = jnp.zeros((group, roundup(cols + 2, 128) - cols - 2), F32)
    same = jnp.concatenate([chip[:, :cols], tail, spare], axis=1)
    cross = jnp.concatenate([chip[:, cols : 2 * cols], tail, spare], axis=1)
    same, cross, x = lax.optimization_barrier((same, cross, x))
    parts = [same, swap(same, 1, 0, 0), swap(cross, 0, 1, 0), swap(cross, 1, 1, 0)]

    share = width // XH // Y
    (x,) = call(
        turn_kernel,
        6,
        [((roundup(Y * share, 128), rows + 2 * group), BF16)],
        [],
        0,
        rows * width * 2,
        x,
    )
    x, *dv = lax.optimization_barrier((x, *dv))
    packed = roundup(3 * cols + 3, 128)
    terms = call(
        weight_kernel,
        16,
        [((share, packed), BF16)] * Y,
        [
            pltpu.VMEM((rows + 2 * group, 3 * wide), BF16),
            pltpu.VMEM((roundup(Y * share, 128), 3 * wide), F32),
            pltpu.VMEM((group, wide), F32),
            pltpu.VMEM((share, packed), F32),
            pltpu.VMEM((FRAMES, group, wide), F32),
            pltpu.SemaphoreType.DMA(()),
        ],
        6 * rows * Y * share * cols,
        rows * width * 2,
        *parts,
        unit,
        pnorm,
        slope,
        x,
        loose={6: pltpu.HBM},
    )
    dv = [dv[0]] + [move(dv[i], i, 0) for i in range(1, Y)]
    *dv, first = lax.optimization_barrier((*dv, terms[1]))
    terms = [terms[0], first, *terms[2:]]
    (dv,) = call(
        functools.partial(caption_y_kernel, cap_dev),
        6,
        [((Z, 2 * cap_dev, width), BF16)],
        [],
        2 * count * group * width,
        count * width * 4,
        *dv,
    )
    terms = [terms[0]] + [move(terms[i], i, 0) for i in range(1, Y)]
    own_rows = share // Z
    kept = own_rows // 16 * 16
    (terms,) = call(
        functools.partial(along_y_kernel, 3 * cols),
        8,
        [((Z, kept, packed + 128 + width), BF16)],
        [pltpu.VMEM((share, packed), F32), pltpu.VMEM((Z, kept, packed + 128), F32)],
        0,
        share * packed * 16,
        *terms,
        dv,
    )
    terms = exchange(terms, Z_GROUPS)
    grad_weight, loss, grad_captions = call(
        functools.partial(along_z_kernel, packed, packed + 128),
        4,
        [((3, own_rows, cols), F32), ((1, 1), F32), ((cap_dev, width), F32)],
        [pltpu.VMEM((roundup(own_rows, 8), packed + 128 + width), F32), pltpu.VMEM((cap_dev, width), F32)],
        0,
        share * packed * 2,
        terms,
        captions,
    )
    loss = loss[0, 0] / (clip_dev * lax.axis_size("clip"))
    return (loss, grad_weight, grad_captions)


def solution(mesh):
    placed = (P("clip", "frame", None), P(), P(("clip", "frame"), None), P("clip"))
    return jax.shard_map(
        on_device,
        mesh=mesh,
        in_specs=placed,
        out_specs=(P(), P(None, "clip", "frame"), P(("clip", "frame"), None)),
        check_vma=False,
    )
```
